512 devices in a mesh: lat: 16 (over z_hi, x, core), lon: 32 (over y, z_lo).
Axes of the slice: x: 4, y: 8, z: 8 (z_hi: 2, z_lo: 4; z = z_hi * 4 + z_lo), core: 2. Of those that a mesh axis runs over, the one named last changes fastest.
Arguments:
- tokens: bfloat16 [4, 96, 384, 512], P(None, 'lat', 'lon'), may hold values from -6 to 6
- cotangent: bfloat16 [4, 96, 384, 512], P(None, 'lat', 'lon'), may hold values from -6 to 6
- w_qkv: bfloat16 [512, 1536], replicated, may hold values from -1.06066017 to 1.06066017
- w_out: bfloat16 [512, 512], replicated, may hold values from -1 to 1
- land_mask: int32 [96, 384], replicated, may hold values 0 or 1
- land_bias: float32 [8], replicated, may hold values from -2 to 2
Outputs:
- attended: bfloat16 [4, 96, 384, 512], P(None, 'lat', 'lon')
- grad_tokens: bfloat16 [4, 96, 384, 512], P(None, 'lat', 'lon')
- grad_qkv: float32 [512, 1536], P('lat', 'lon')
- grad_out: float32 [512, 512], P('lat', 'lon')
- grad_bias: float32 [8], replicated
The draws below stay inside these ranges and needn't reach their ends.
All inputs are finite; a program needn't handle non-finite values.
Results may differ from the reference program's by a relative error of at most 0.034.
The reference program's roundings to bfloat16 on the way count: a program that leaves them out, or rounds other values in their place, can miss the bound.
Values may be sent and summed in bfloat16 or wider, within the bound.
A program may use at most 64 MiB of HBM per device.

```python
import jax
import jax.numpy as jnp
from jax import lax

D = 512
HEADS = 8
HEAD = 64
WLAT = 6
WLON = 12
LEV = 4
NLAT = 96
NLON = 384


def draw_tokens(key, part):
    key = jax.random.fold_in(key, 11)
    base = jax.random.truncated_normal(key, -6.0, 6.0, (LEV, NLAT, NLON, D), jnp.float32)
    return base.astype(jnp.bfloat16)


def draw_w_qkv(key, part):
    key = jax.random.fold_in(key, 23)
    query_key, other_key, value_key, order_key = jax.random.split(key, 4)
    scale = D ** (-0.5)
    query_base = jax.random.truncated_normal(query_key, -3.0, 3.0, (D, D), jnp.float32)
    other_base = jax.random.truncated_normal(other_key, -3.0, 3.0, (D, D), jnp.float32)
    value_base = jax.random.truncated_normal(value_key, -3.0, 3.0, (D, D), jnp.float32)
    order = jax.random.permutation(order_key, HEADS).astype(jnp.float32)
    strength = 0.8 * jnp.power(2.0, order / max(HEADS - 1, 1))
    column_scale = jnp.repeat(strength, HEAD) * scale
    w_query = query_base * column_scale[None, :]
    w_key = other_base * column_scale[None, :]
    w_value = value_base * scale
    return jnp.concatenate([w_query, w_key, w_value], axis=1).astype(jnp.bfloat16)


def plant(array, key, low, top_value):
    longest = array.shape.index(max(array.shape))
    spots = []
    for shift in (0, 1):
        where = [jax.random.randint(jax.random.fold_in(key, axis), (), 0, length) for axis, length in enumerate(array.shape)]
        where[longest] = (where[longest] + shift) % array.shape[longest]
        spots.append(tuple(where))
    return array.at[spots[0]].set(low).at[spots[1]].set(top_value)


def shard_levels(rng, dims, cuts, smallest, largest):
    level = 1.0
    for axis_at, blocks in cuts:
        heights = jax.random.uniform(jax.random.fold_in(jax.random.fold_in(rng, 6), axis_at), (blocks,), jnp.float32, smallest / len(cuts), largest / len(cuts))
        level = level * jnp.repeat(jnp.exp(heights), dims[axis_at] // blocks).reshape((-1,) + (1,) * (len(dims) - 1 - axis_at))
    return level


def scatter_about(own_key, shape, deviation, limit, cuts=(), kind=jnp.bfloat16):
    loudness = shard_levels(own_key, shape, cuts, -0.22, 0.18) if cuts else 1.0
    result = jax.random.normal(own_key, shape, jnp.float32) * deviation * loudness
    return jnp.minimum(jnp.maximum(result, -limit), limit).astype(kind)


def setup_inputs(seed: int = 0) -> dict:
    splits = jax.random.split(jax.random.key(seed), 7)
    tokens = draw_tokens(jax.random.fold_in(splits[6], 71), 0)
    cotangent = scatter_about(splits[1], (LEV, NLAT, NLON, D), 1.0, 6.0, ((1, 16), (2, 32)))
    w_qkv = draw_w_qkv(jax.random.fold_in(splits[6], 71), 0)
    w_out = scatter_about(splits[3], (D, D), (D // 16) ** -0.5, 1.0)
    land_mask = plant((jax.random.randint(splits[4], (NLAT, NLON), 0, 3) < 1).astype(jnp.int32), jax.random.fold_in(splits[4], 1), 0, 1)
    land_bias = jnp.clip(jax.random.uniform(splits[5], (HEADS,), jnp.float32, -2.0, 2.0), -2.0, 2.0)
    return {"tokens": tokens, "cotangent": cotangent, "w_qkv": w_qkv, "w_out": w_out, "land_mask": land_mask, "land_bias": land_bias}


def layer_norm(tokens_f):
    mean_value = lax.optimization_barrier(jnp.mean(tokens_f, axis=-1, keepdims=True))
    centred = tokens_f - mean_value
    variance = lax.optimization_barrier(jnp.mean(centred * centred, axis=-1, keepdims=True))
    inv_scale = lax.rsqrt(variance + 1e-05)
    return (centred * inv_scale, inv_scale)

def window_split(grid):
    level_count, lat_rows, lon_cols, features = grid.shape
    grid = grid.reshape(level_count // 2, 2, lat_rows // WLAT, WLAT, lon_cols // WLON, WLON, features)
    grid = grid.transpose(0, 2, 4, 1, 3, 5, 6)
    return grid.reshape(-1, 2 * WLAT * WLON, features)

def window_merge(windows, level_count, lat_rows, lon_cols):
    features = windows.shape[-1]
    grid = windows.reshape(level_count // 2, lat_rows // WLAT, lon_cols // WLON, 2, WLAT, WLON, features)
    grid = grid.transpose(0, 3, 1, 4, 2, 5, 6)
    return grid.reshape(level_count, lat_rows, lon_cols, features)

def window_attention(qkv, land, region, land_bias):
    block_count, win_len = (qkv.shape[0], qkv.shape[1])
    head_count = land_bias.shape[0]
    head_size = qkv.shape[2] // (3 * head_count)
    split_qkv = qkv.reshape(block_count, win_len, 3, head_count, head_size)
    queries = split_qkv[:, :, 0].astype(jnp.float32)
    key_vecs = split_qkv[:, :, 1].astype(jnp.float32)
    values_f = split_qkv[:, :, 2].astype(jnp.float32)
    scores = jnp.einsum('bqhd,bkhd->bhqk', queries, key_vecs) * head_size ** (-0.5)
    scores = scores + land_bias[None, :, None, None] * land.astype(jnp.float32)[:, None, None, :]
    same_region = region[:, :, None] == region[:, None, :]
    scores = jnp.where(same_region[:, None], scores, -1e+30)
    peak_score = lax.optimization_barrier(jnp.max(scores, axis=-1, keepdims=True))
    expo = jnp.exp(scores - peak_score)
    weights_bf = (expo / lax.optimization_barrier(jnp.sum(expo, axis=-1, keepdims=True))).astype(jnp.bfloat16)
    mixed = jnp.einsum('bhqk,bkhd->bqhd', weights_bf.astype(jnp.float32), values_f)
    return mixed.reshape(block_count, win_len, head_count * head_size).astype(jnp.bfloat16)

def window_pass(tokens, grad_in, land, region, w_qkv, w_out, land_bias):
    block_count, win_len, features = tokens.shape
    normal, inv_scale = layer_norm(tokens.astype(jnp.float32))
    flat_normed = normal.astype(jnp.bfloat16).reshape(block_count * win_len, features)
    qkv = jnp.dot(flat_normed, w_qkv, preferred_element_type=jnp.float32).astype(jnp.bfloat16)
    qkv = qkv.reshape(block_count, win_len, 3 * features)

    def attend(qkv_in, bias_in):
        return window_attention(qkv_in, land, region, bias_in)
    mixed, pullback = jax.vjp(attend, qkv, land_bias)
    mixed_flat = mixed.reshape(block_count * win_len, features)
    attended = jnp.dot(mixed_flat, w_out, preferred_element_type=jnp.float32).astype(jnp.bfloat16)
    grad_flat = grad_in.reshape(block_count * win_len, features)
    d_mixed = jnp.dot(grad_flat, w_out.T, preferred_element_type=jnp.float32).astype(jnp.bfloat16)
    d_wout = jnp.dot(mixed_flat.T, grad_flat, preferred_element_type=jnp.float32)
    d_qkv, d_bias = pullback(d_mixed.reshape(block_count, win_len, features))
    d_qkv_flat = d_qkv.reshape(block_count * win_len, 3 * features)
    d_wqkv = jnp.dot(flat_normed.T, d_qkv_flat, preferred_element_type=jnp.float32)
    d_normed = jnp.dot(d_qkv_flat, w_qkv.T, preferred_element_type=jnp.float32)
    d_normed = d_normed.reshape(block_count, win_len, features)
    mean_grad = lax.optimization_barrier(jnp.mean(d_normed, axis=-1, keepdims=True))
    mean_cross = lax.optimization_barrier(jnp.mean(d_normed * normal, axis=-1, keepdims=True))
    d_tokens = (inv_scale * (d_normed - mean_grad - normal * mean_cross)).astype(jnp.bfloat16)
    return (attended.reshape(block_count, win_len, features), d_tokens, d_wqkv, d_wout, d_bias)

def reference(tokens, cotangent, w_qkv, w_out, land_mask, land_bias):
    half_lat = WLAT // 2
    half_lon = WLON // 2
    win_len = 2 * WLAT * WLON
    rolled = window_split(jnp.roll(tokens, (-1, -half_lat, -half_lon), (0, 1, 2)))
    rolled_cot = window_split(jnp.roll(cotangent, (-1, -half_lat, -half_lon), (0, 1, 2)))
    land_grid = jnp.roll(land_mask, (-half_lat, -half_lon), (0, 1))
    land_grid = jnp.broadcast_to(land_grid[None, :, :, None], (LEV, NLAT, NLON, 1))
    land_win = window_split(land_grid)[..., 0]
    lat_flag = (jnp.arange(NLAT) >= NLAT - half_lat).astype(jnp.int32)
    level_flag = (jnp.arange(LEV) == LEV - 1).astype(jnp.int32)
    region_grid = 2 * lat_flag[None, :, None] + level_flag[:, None, None] + jnp.zeros((LEV, NLAT, NLON), jnp.int32)
    region_win = window_split(region_grid[..., None])[..., 0]
    group_count = LEV // 2 * (NLAT // WLAT)

    def one_group(pieces):
        return window_pass(pieces[0], pieces[1], pieces[2], pieces[3], w_qkv, w_out, land_bias)
    outs = lax.map(one_group, (rolled.reshape(group_count, -1, win_len, D), rolled_cot.reshape(group_count, -1, win_len, D), land_win.reshape(group_count, -1, win_len), region_win.reshape(group_count, -1, win_len)))
    attended_w = outs[0].reshape(-1, win_len, D)
    d_tokens_w = outs[1].reshape(-1, win_len, D)
    grad_qkv = lax.optimization_barrier(jnp.sum(outs[2], axis=0))
    grad_out = lax.optimization_barrier(jnp.sum(outs[3], axis=0))
    grad_bias = lax.optimization_barrier(jnp.sum(outs[4], axis=0))
    attended = jnp.roll(window_merge(attended_w, LEV, NLAT, NLON), (1, half_lat, half_lon), (0, 1, 2))
    grad_tokens = jnp.roll(window_merge(d_tokens_w, LEV, NLAT, NLON), (1, half_lat, half_lon), (0, 1, 2))
    return (attended, grad_tokens, grad_qkv, grad_out, grad_bias)
```

```python
import jax
import jax.numpy as jnp
from jax import lax
from jax.experimental import pallas as pl
from jax.experimental.pallas import tpu as pltpu
from jax.sharding import PartitionSpec as P

MESH = pl.DeviceIdType.MESH
BF = jnp.bfloat16
F32 = jnp.float32
D = 512
HEADS = 8
HD = 64
WIN = 144
PART = 36
QROWS = 80
NX, NY, NZ = 4, 8, 8


def nn(a, b):
    return lax.dot_general(a, b, (((1,), (0,)), ((), ())), preferred_element_type=F32)


def nt(a, b):
    return lax.dot_general(a, b, (((1,), (1,)), ((), ())), preferred_element_type=F32)


def tn(a, b):
    return lax.dot_general(a, b, (((0,), (0,)), ((), ())), preferred_element_type=F32)


def iota(shape, axis):
    return lax.broadcasted_iota(jnp.int32, shape, axis)


def one_hot(cond):
    return jnp.where(cond, 1.0, 0.0).astype(BF)


def token_place(t):
    quad = (t >= 36).astype(jnp.int32) + (t >= 72).astype(jnp.int32) + (t >= 108).astype(jnp.int32)
    rem = t - 36 * quad
    lev = (rem >= 18).astype(jnp.int32)
    pos = rem - 18 * lev
    row = (pos >= 6).astype(jnp.int32) + (pos >= 12).astype(jnp.int32)
    return quad, lev, row, pos - 6 * row


def quad_row(s):
    w = (s >= WIN).astype(jnp.int32)
    t = s - WIN * w
    quad = (t >= 36).astype(jnp.int32) + (t >= 72).astype(jnp.int32) + (t >= 108).astype(jnp.int32)
    return quad * QROWS + w * PART + (t - 36 * quad)


def kernel(
    xq, cq, wqkv_h, wout_h, land, bias,
    out_att, out_tok, g_qkv, g_out, g_bias,
    hx, hc, wqkv, wout, wt, perm, sel, selt, normal, inv,
    normw, cotw, nmt, qkvt, dmt, mixt, mixp, dqkvt, r_q, r_o,
    oa, ot, core_s, core_r,
    a1, ra1, a2, ra2, a3, ra3, b1, rb1, b2, rb2, b3, rb3, c1, rc1, c2, rc2, c3, rc3,
    dbias, bc, bx, by, bz,
    lsem, hs, hr, os, orr, cs, cr, xs, xr, ys, yr, zs, zr,
):
    lat = lax.axis_index("lat")
    lon = lax.axis_index("lon")
    core = lat & 1
    px = (lat >> 1) & 3
    pzh = lat >> 3
    py = lon >> 2
    pzl = lon & 3
    pz = pzh * 4 + pzl

    def dev(x, y, z, c):
        return ((z >> 2) * 8 + x * 2 + c, y * 4 + (z & 3))

    def at_core():
        return dev(px, py, pz, 1 - core)

    def at_x(d):
        return dev((px + d) & 3, py, pz, core)

    def at_y(d):
        return dev(px, (py + d) & 7, pz, core)

    def at_z(d):
        return dev(px, py, (pz + d) & 7, core)

    back = [None, ((lat + 15) & 15, lon), (lat, (lon + 31) & 31), ((lat + 15) & 15, (lon + 31) & 31)]
    ahead = [None, ((lat + 1) & 15, lon), (lat, (lon + 1) & 31), ((lat + 1) & 15, (lon + 1) & 31)]

    w_copy = pltpu.make_async_copy(wqkv_h, wqkv, lsem.at[0])
    w_copy.start()
    o_copy = pltpu.make_async_copy(wout_h, wout, lsem.at[1])
    o_copy.start()

    barrier = pltpu.get_barrier_semaphore()
    partners = back[1:] + ahead[1:] + [at_core()]
    partners += [at_x(d) for d in range(1, NX)]
    partners += [at_y(d) for d in range(1, NY)] + [at_z(d) for d in range(1, NZ)]
    for where in partners:
        pl.semaphore_signal(barrier, inc=1, device_id=where, device_id_type=MESH)
    pl.semaphore_wait(barrier, len(partners))

    def send(src, dst, ssem, rsem, where):
        copy = pltpu.make_async_remote_copy(
            src_ref=src, dst_ref=dst, send_sem=ssem, recv_sem=rsem,
            device_id=where, device_id_type=MESH,
        )
        copy.start()
        return copy

    halo_x = [send(xq.at[q], hx.at[q - 1], hs.at[q - 1], hr.at[q - 1], back[q]) for q in (3, 1, 2)]
    halo_c = [send(cq.at[q], hc.at[q - 1], hs.at[q + 2], hr.at[q + 2], back[q]) for q in (3, 1, 2)]

    s_col = iota((2 * WIN, 1), 0)
    sel[...] = one_hot(iota((2 * WIN, 4 * QROWS), 1) == quad_row(s_col))
    for w in range(2):
        s_row = iota((1, WIN), 1) + w * WIN
        selt[w] = one_hot(iota((4 * QROWS, WIN), 0) == quad_row(s_row))
    r = iota((D, 1), 0)
    half = r >> 8
    a = r & 255
    is_a = a < 128
    is_b = a < 192
    b = a & 63
    f_x = jnp.where(is_a, a >> 5, jnp.where(is_b, b >> 4, (b >> 3) & 3))
    f_zh = jnp.where(is_a, (a >> 4) & 1, jnp.where(is_b, (b >> 3) & 1, b >> 5))
    f_i = jnp.where(is_a, a & 15, jnp.where(is_b, 16 + (b & 7), 24 + (b & 7)))
    f_c = jnp.where(half == 0, 1 - core, core)
    perm[...] = one_hot(iota((D, D), 1) == f_zh * 256 + f_x * 64 + f_c * 32 + f_i)
    r_q[...] = jnp.zeros_like(r_q)
    r_o[...] = jnp.zeros_like(r_o)

    quad, _, row, col = token_place(iota((WIN, 1), 0))
    l_row = lat * 6 + 3 + (quad & 1) * 3 + row
    l_row = jnp.where(l_row >= 96, l_row - 96, l_row)
    l_col = lon * 12 + 6 + (quad >> 1) * 6 + col
    l_col = jnp.where(l_col >= 384, l_col - 384, l_col)
    picked = nn(one_hot(iota((WIN, 96), 1) == l_row), land[...].astype(F32).astype(BF))
    land_key = jnp.sum(jnp.where(iota((WIN, 384), 1) == l_col, picked, 0.0), axis=1, keepdims=True)

    def region(t, w):
        quad, lev, _, _ = token_place(t)
        seam = jnp.where(lat == 15, 2, 0)
        return seam * (quad & 1) + (lev if w == 1 else 0)

    masks = [
        jnp.where(region(iota((WIN, 1), 0), w) == region(iota((1, WIN), 1), w), 0.0, -1e30)
        for w in range(2)
    ]

    w_copy.wait()
    o_copy.wait()
    eye = one_hot(iota((256, 256), 0) == iota((256, 256), 1))
    for k in range(6):
        wt[256 * k : 256 * k + 256] = nt(eye, wqkv[:, 256 * k : 256 * k + 256]).astype(BF)

    def layer_norm(x, q):
        x = x.astype(F32)
        centred = x - jnp.mean(x, axis=1, keepdims=True)
        scale = lax.rsqrt(jnp.mean(centred * centred, axis=1, keepdims=True) + 1e-05)
        normal[q] = centred * scale
        inv[q] = jnp.broadcast_to(scale, (QROWS, 128))

    layer_norm(xq[0], 0)
    for copy, q in zip(halo_x, (3, 1, 2)):
        copy.wait()
        layer_norm(hx[q - 1], q)
    normed = normal[...].reshape(4 * QROWS, D).astype(BF)
    normw[...] = nn(sel[...], normed).astype(BF)
    for w in range(2):
        nw = normw[WIN * w : WIN * w + WIN]
        qkvt[w] = nt(wt[...], nw).astype(BF)
        nmt[w] = nt(perm[...], nw).astype(BF)
    for copy in halo_c:
        copy.wait()
    cot = jnp.concatenate([cq[0], hc[0], hc[1], hc[2]], axis=0)
    cotw[...] = nn(sel[...], cot).astype(BF)
    for w in range(2):
        cw = cotw[WIN * w : WIN * w + WIN]
        dmt[w] = nt(wout[...], cw).astype(BF)
        for k in range(2):
            ct = nt(eye, cw[:, 256 * k : 256 * k + 256]).astype(BF)
            for g in range(16):
                at = 64 * (16 * k + g) + 48
                r_o[w, at : at + 16] = ct[16 * g : 16 * g + 16]

    def one_head(h, carry):
        base = pl.multiple_of(h * HD, HD)
        bias_h = bias[h]
        d_bias = jnp.zeros((1, WIN), F32)
        for w in range(2):
            qt = qkvt[w, pl.ds(base, HD)]
            kt = qkvt[w, pl.ds(D + base, HD)]
            vt = qkvt[w, pl.ds(2 * D + base, HD)]
            dm = dmt[w, pl.ds(base, HD)]
            score = tn(kt, qt) * (HD ** -0.5) + (bias_h * land_key + masks[w])
            expo = jnp.exp(score - jnp.max(score, axis=0, keepdims=True))
            prob = expo * (1.0 / jnp.sum(expo, axis=0, keepdims=True))
            prob_b = prob.astype(BF)
            mixt[w, pl.ds(base, HD)] = nn(vt, prob_b).astype(BF)
            d_prob = tn(vt, dm).astype(BF).astype(F32)
            d_v = nt(dm, prob_b).astype(BF)
            d_score = prob * (d_prob - jnp.sum(prob * d_prob, axis=0, keepdims=True))
            d_bias = d_bias + jnp.sum(d_score * land_key, axis=0, keepdims=True)
            ds_b = d_score.astype(BF)
            d_q = (nn(kt, ds_b) * (HD ** -0.5)).astype(BF)
            d_k = (nt(qt, ds_b) * (HD ** -0.5)).astype(BF)
            for part, grad in enumerate((d_q, d_k, d_v)):
                dqkvt[w, pl.ds(part * D + base, HD)] = grad
                for g in range(4):
                    piece = h * 4 + (part * 32 + g)
                    at = pl.multiple_of((piece // 3) * 64 + (piece % 3) * 16, 16)
                    r_q[w, pl.ds(at, 16)] = grad[16 * g : 16 * g + 16]
        dbias[pl.ds(h, 1)] = d_bias
        return carry

    lax.fori_loop(0, HEADS, one_head, 0)

    bc[0] = jnp.broadcast_to(jnp.sum(dbias[...], axis=1, keepdims=True), (HEADS, 128))
    bias_c = send(bc.at[0], bc.at[1], cs.at[0], cr.at[0], at_core())

    for w in range(2):
        mixp[w] = nn(perm[...], mixt[w]).astype(BF)

    def grad_block(first, y):
        cols = pl.ds(pl.multiple_of(y * 256, 256), 256)
        total = None
        for w in range(2):
            for left, right in ((nmt, r_q), (mixp, r_o)):
                term = nt(left[w, first : first + 256], right[w, cols])
                total = term if total is None else total + term
        return total

    def partner_block(y, carry):
        core_s[y] = grad_block(0, y).astype(BF)
        return carry

    lax.fori_loop(0, NY, partner_block, 0)
    core_copy = send(core_s, core_r, cs.at[1], cr.at[1], at_core())

    core_copy.wait()
    lane_low = iota((64, 128), 1) < 64
    kept = []
    for y in range(NY):
        total = grad_block(256, y) + core_r[y].astype(F32)
        for x in range(NX):
            a1[x, y] = total[32 * x : 32 * x + 32].astype(BF)
        b1[y] = total[128:192].astype(BF)
        kept.append(total[192:256])
        if y % 2 == 1:
            m = y // 2
            for t in range(2):
                lo = kept[0][:, 128 * t : 128 * t + 128]
                hi = kept[1][:, 128 * t : 128 * t + 128]
                even = jnp.where(lane_low, lo, pltpu.roll(hi, 64, 1)).astype(BF)
                odd = jnp.where(lane_low, pltpu.roll(lo, 64, 1), hi).astype(BF)
                for zh in range(2):
                    c1[zh * 4 + 2 * t, :, 128 * m : 128 * m + 128] = even[32 * zh : 32 * zh + 32]
                    c1[zh * 4 + 2 * t + 1, :, 128 * m : 128 * m + 128] = odd[32 * zh : 32 * zh + 32]
            kept = []

    def swap_x(src, dst, stage):
        return [send(src(d), dst.at[d - 1], xs.at[stage, d - 1], xr.at[stage, d - 1], at_x(d)) for d in (2, 1, 3)]

    def swap_y(src, dst, stage):
        return [send(src(d), dst.at[d - 1], ys.at[stage, d - 1], yr.at[stage, d - 1], at_y(d)) for d in (4, 3, 5, 2, 6, 1, 7)]

    def swap_z(src, dst, stage):
        return [send(src(d), dst.at[d - 1], zs.at[stage, d - 1], zr.at[stage, d - 1], at_z(d)) for d in (4, 3, 5, 2, 6, 1, 7)]

    def wait(copies):
        for copy in copies:
            copy.wait()

    def summed(own_part, parts, count):
        total = own_part.astype(F32)
        for d in range(count):
            total = total + parts[d].astype(F32)
        return total

    go_a = swap_x(lambda d: a1.at[(px + d) & 3], ra1, 0)
    go_b = swap_y(lambda d: b1.at[(py + d) & 7], rb1, 0)
    go_c = swap_z(lambda d: c1.at[(pz + d) & 7], rc1, 0)
    bias_c.wait()
    bx[0] = bc[0] + bc[1]
    go_bias = [send(bx.at[0], bx.at[d], xs.at[3, d - 1], xr.at[3, d - 1], at_x(d)) for d in (2, 1, 3)]

    out_sends = []
    for q in (3, 1, 2, 0):
        rows = slice(QROWS * q, QROWS * q + QROWS)
        mixed = (nt(selt[0, rows], mixt[0]) + nt(selt[1, rows], mixt[1])).astype(BF)
        att = nn(mixed, wout[...]).astype(BF)
        if q == 0:
            out_att[0] = att
        else:
            oa[q - 1] = att
            out_sends.append(send(oa.at[q - 1], out_att.at[q], os.at[q - 1], orr.at[q - 1], ahead[q]))
        d_qkv = (nt(selt[0, rows], dqkvt[0]) + nt(selt[1, rows], dqkvt[1])).astype(BF)
        d_normed = nn(d_qkv, wt[...])
        norm = normal[q]
        mean_grad = jnp.mean(d_normed, axis=1, keepdims=True)
        mean_cross = jnp.mean(d_normed * norm, axis=1, keepdims=True)
        d_tok = (inv[q][:, 0:1] * (d_normed - mean_grad - norm * mean_cross)).astype(BF)
        if q == 0:
            out_tok[0] = d_tok
        else:
            ot[q - 1] = d_tok
            out_sends.append(send(ot.at[q - 1], out_tok.at[q], os.at[q + 2], orr.at[q + 2], ahead[q]))

    wait(go_a)
    for y in range(NY):
        total = a1[px, y].astype(F32)
        for d in range(3):
            total = total + ra1[d, y].astype(F32)
        a2[y] = total.astype(BF)
    go_a = swap_y(lambda d: a2.at[(py + d) & 7], ra2, 1)
    wait(go_b)
    total = summed(b1[py], rb1, 7)
    for zh in range(2):
        for t in range(2):
            for x in range(NX):
                at = 16 * x + 8 * zh
                b2[zh * 2 + t, 8 * x : 8 * x + 8] = total[at : at + 8, 128 * t : 128 * t + 128]
    go_b = swap_z(lambda d: b2.at[((pz + d) & 7) >> 1], rb2, 1)
    wait(go_c)
    total = summed(c1[pz], rc1, 7)
    for x in range(NX):
        c2[x] = total[8 * x : 8 * x + 8]
    go_c = swap_x(lambda d: c2.at[(px + d) & 3], rc2, 1)
    wait(go_bias)

    def ordered(slots, me, n):
        total = slots[me & (n - 1)]
        for k in range(1, n):
            total = total + slots[(me - k) & (n - 1)]
        return total

    by[0] = ordered(bx, px, NX)
    go_bias = [send(by.at[0], by.at[d], ys.at[3, d - 1], yr.at[3, d - 1], at_y(d)) for d in (4, 3, 5, 2, 6, 1, 7)]

    wait(go_a)
    total = summed(a2[py], ra2, 7)
    for zh in range(2):
        for t in range(2):
            a3[zh * 2 + t] = total[16 * zh : 16 * zh + 16, 128 * t : 128 * t + 128]
    go_a = swap_z(lambda d: a3.at[((pz + d) & 7) >> 1], ra3, 2)
    wait(go_b)
    total = summed(b2[pz >> 1], rb2, 7)
    for x in range(NX):
        b3[x] = total[8 * x : 8 * x + 8]
    go_b = swap_x(lambda d: b3.at[(px + d) & 3], rb3, 2)
    wait(go_c)
    total = summed(c2[px], rc2, 3)
    for m in range(4):
        c3[m] = total[:, 128 * m : 128 * m + 128]
    go_c = swap_y(lambda d: c3.at[((py + d) & 7) >> 1], rc3, 2)
    wait(go_bias)
    bz[0] = ordered(by, py, NY)
    go_bias = [send(bz.at[0], bz.at[d], zs.at[3, d - 1], zr.at[3, d - 1], at_z(d)) for d in (4, 3, 5, 2, 6, 1, 7)]

    def mine(total, odd):
        return jnp.where(odd == 1, pltpu.roll(total, 64, 1), total)

    def put(first, total):
        count = total.shape[0]
        g_qkv[first : first + count] = total[:, 0:48]
        g_out[first : first + count] = total[:, 48:64]

    wait(go_a)
    put(0, mine(summed(a3[pz >> 1], ra3, 7), pzl & 1))
    wait(go_b)
    put(16, mine(summed(b3[px], rb3, 3), pzl & 1))
    wait(go_c)
    put(24, mine(summed(c3[py >> 1], rc3, 7), py & 1))
    wait(go_bias)
    g_bias[...] = ordered(bz, pz, NZ)
    wait(out_sends)


def to_quads(grid):
    moved = jnp.concatenate([grid[1:], grid[:1]], axis=0)
    quads = []
    for lon_part in (1, 0):
        for lat_part in (1, 0):
            block = moved[:, 3 * lat_part : 3 * lat_part + 3, 6 * lon_part : 6 * lon_part + 6]
            quads.append(jnp.pad(block.reshape(72, D), ((0, QROWS - 72), (0, 0))))
    return jnp.stack(quads)


def from_quads(quads):
    q = quads[:, :72].reshape(4, 4, 3, 6, D)
    high = jnp.concatenate([q[3], q[1]], axis=2)
    low = jnp.concatenate([q[2], q[0]], axis=2)
    grid = jnp.concatenate([high, low], axis=1)
    return jnp.concatenate([grid[3:], grid[:3]], axis=0)


def shards(tokens, cotangent, w_qkv, w_out, land_mask, land_bias):
    vmem = pl.BlockSpec(memory_space=pltpu.VMEM)
    anywhere = pl.BlockSpec(memory_space=pl.ANY)
    V = pltpu.VMEM
    dma = pltpu.SemaphoreType.DMA
    att, tok, g_qkv, g_out, g_bias = pl.pallas_call(
        kernel,
        out_shape=[
            jax.ShapeDtypeStruct((4, QROWS, D), BF),
            jax.ShapeDtypeStruct((4, QROWS, D), BF),
            jax.ShapeDtypeStruct((32, 48), F32),
            jax.ShapeDtypeStruct((32, 16), F32),
            jax.ShapeDtypeStruct((HEADS, 128), F32),
        ],
        in_specs=[vmem, vmem, anywhere, anywhere, vmem, pl.BlockSpec(memory_space=pltpu.SMEM)],
        out_specs=[vmem] * 5,
        scratch_shapes=[
            V((3, QROWS, D), BF), V((3, QROWS, D), BF),
            V((D, 3 * D), BF), V((D, D), BF), V((3 * D, D), BF),
            V((D, D), BF), V((2 * WIN, 4 * QROWS), BF), V((2, 4 * QROWS, WIN), BF),
            V((4, QROWS, D), F32), V((4, QROWS, 128), F32),
            V((2 * WIN, D), BF), V((2 * WIN, D), BF),
            V((2, D, WIN), BF), V((2, 3 * D, WIN), BF), V((2, D, WIN), BF),
            V((2, D, WIN), BF), V((2, D, WIN), BF), V((2, 3 * D, WIN), BF),
            V((2, 4 * D, WIN), BF), V((2, 4 * D, WIN), BF),
            V((3, QROWS, D), BF), V((3, QROWS, D), BF),
            V((NY, 256, 256), BF), V((NY, 256, 256), BF),
            V((NX, NY, 32, 256), BF), V((3, NY, 32, 256), BF),
            V((NY, 32, 256), BF), V((7, 32, 256), BF),
            V((4, 16, 128), F32), V((7, 16, 128), F32),
            V((NY, 64, 256), BF), V((7, 64, 256), BF),
            V((4, 32, 128), F32), V((7, 32, 128), F32),
            V((NX, 8, 128), F32), V((3, 8, 128), F32),
            V((NZ, 32, 512), BF), V((7, 32, 512), BF),
            V((NX, 8, 512), F32), V((3, 8, 512), F32),
            V((4, 8, 128), F32), V((7, 8, 128), F32),
            V((HEADS, WIN), F32), V((2, HEADS, 128), F32),
            V((NX, HEADS, 128), F32), V((NY, HEADS, 128), F32), V((NZ, HEADS, 128), F32),
            dma((2,)), dma((6,)), dma((6,)), dma((6,)), dma((6,)),
            dma((2,)), dma((2,)),
            dma((4, 3)), dma((4, 3)), dma((4, 7)), dma((4, 7)), dma((4, 7)), dma((4, 7)),
        ],
        compiler_params=pltpu.CompilerParams(
            collective_id=0, has_side_effects=True, vmem_limit_bytes=48 << 20
        ),
        name="swin_block",
    )(to_quads(tokens), to_quads(cotangent), w_qkv, w_out, land_mask, land_bias)
    return from_quads(att), from_quads(tok), g_qkv, g_out, g_bias[:, 0]


def solution(mesh):
    in_specs = (P(None, "lat", "lon", None), P(None, "lat", "lon", None), P(), P(), P(), P())
    out_specs = (
        P(None, "lat", "lon", None),
        P(None, "lat", "lon", None),
        P("lat", "lon"),
        P("lat", "lon"),
        P(),
    )
    return jax.shard_map(shards, mesh=mesh, in_specs=in_specs, out_specs=out_specs, check_vma=False)
```

```python
import jax
import jax.numpy as jnp
from jax import lax
from jax.experimental import pallas as pl
from jax.experimental.pallas import tpu as pltpu
from jax.sharding import PartitionSpec as P

MESH = pl.DeviceIdType.MESH
BF = jnp.bfloat16
F32 = jnp.float32
D = 512
HEADS = 8
HD = 64
WIN = 144
PART = 36
CELLS = 72
PADDED = CELLS * 16
QROWS = 80
NX, NY, NZ = 4, 8, 8


def nn(a, b):
    return lax.dot_general(a, b, (((1,), (0,)), ((), ())), preferred_element_type=F32)


def nt(a, b):
    return lax.dot_general(a, b, (((1,), (1,)), ((), ())), preferred_element_type=F32)


def tn(a, b):
    return lax.dot_general(a, b, (((0,), (0,)), ((), ())), preferred_element_type=F32)


def iota(shape, axis):
    return lax.broadcasted_iota(jnp.int32, shape, axis)


def one_hot(cond):
    return jnp.where(cond, 1.0, 0.0).astype(BF)


def token_place(t):
    quad = (t >= 36).astype(jnp.int32) + (t >= 72).astype(jnp.int32) + (t >= 108).astype(jnp.int32)
    rem = t - 36 * quad
    lev = (rem >= 18).astype(jnp.int32)
    pos = rem - 18 * lev
    row = (pos >= 6).astype(jnp.int32) + (pos >= 12).astype(jnp.int32)
    return quad, lev, row, pos - 6 * row


def quad_row(s):
    w = (s >= WIN).astype(jnp.int32)
    t = s - WIN * w
    quad = (t >= 36).astype(jnp.int32) + (t >= 72).astype(jnp.int32) + (t >= 108).astype(jnp.int32)
    return quad * QROWS + w * PART + (t - 36 * quad)


def grid_row(s):
    quad = (s >= QROWS).astype(jnp.int32) + (s >= 2 * QROWS).astype(jnp.int32) + (s >= 3 * QROWS).astype(jnp.int32)
    rem = s - QROWS * quad
    step = (rem >= 18).astype(jnp.int32) + (rem >= 36).astype(jnp.int32) + (rem >= 54).astype(jnp.int32)
    pos = rem - 18 * step
    row = (pos >= 6).astype(jnp.int32) + (pos >= 12).astype(jnp.int32)
    col = pos - 6 * row
    lev = (step + 1) & 3
    at = ((3 * (1 - (quad & 1)) + row) * 12 + 6 * (1 - (quad >> 1)) + col) * 16 + lev
    return jnp.where(rem < 72, at, -1)


def kernel(
    tok_h, cot_h, wqkv_h, wout_h, land, bias,
    out_att, out_tok, g_qkv, g_out, g_bias,
    tok_v, cot_v, raw, xq, cq, hx, hc, att_q, tok_q, spread,
    wqkv, wout, wt, perm, sel, selt, normal, inv,
    normw, cotw, nmt, qkvt, dmt, mixt, mixp, dqkvt, r_q, r_o,
    oa, ot, core_s, core_r,
    a1, ra1, a2, ra2, a3, ra3, b1, rb1, b2, rb2, b3, rb3, c1, rc1, c2, rc2, c3, rc3,
    dbias, bc, bx, by, bz,
    lsem, hs, hr, os, orr, cs, cr, xs, xr, ys, yr, zs, zr,
):
    lat = lax.axis_index("lat")
    lon = lax.axis_index("lon")
    core = lat & 1
    px = (lat >> 1) & 3
    pzh = lat >> 3
    py = lon >> 2
    pzl = lon & 3
    pz = pzh * 4 + pzl

    def dev(x, y, z, c):
        return ((z >> 2) * 8 + x * 2 + c, y * 4 + (z & 3))

    def at_core():
        return dev(px, py, pz, 1 - core)

    def at_x(d):
        return dev((px + d) & 3, py, pz, core)

    def at_y(d):
        return dev(px, (py + d) & 7, pz, core)

    def at_z(d):
        return dev(px, py, (pz + d) & 7, core)

    back = [None, ((lat + 15) & 15, lon), (lat, (lon + 31) & 31), ((lat + 15) & 15, (lon + 31) & 31)]
    ahead = [None, ((lat + 1) & 15, lon), (lat, (lon + 1) & 31), ((lat + 1) & 15, (lon + 1) & 31)]

    barrier = pltpu.get_barrier_semaphore()
    partners = back[1:] + ahead[1:] + [at_core()]
    partners += [at_x(d) for d in range(1, NX)]
    partners += [at_y(d) for d in range(1, NY)] + [at_z(d) for d in range(1, NZ)]
    for where in partners:
        pl.semaphore_signal(barrier, inc=1, device_id=where, device_id_type=MESH)

    t_copy = pltpu.make_async_copy(tok_h, tok_v, lsem.at[2])
    t_copy.start()
    c_copy = pltpu.make_async_copy(cot_h, cot_v, lsem.at[3])
    c_copy.start()
    w_copy = pltpu.make_async_copy(wqkv_h, wqkv, lsem.at[0])
    w_copy.start()
    o_copy = pltpu.make_async_copy(wout_h, wout, lsem.at[1])
    o_copy.start()
    raw[...] = jnp.zeros_like(raw)
    spread[...] = one_hot(iota((PADDED, 4 * QROWS), 0) == grid_row(iota((1, 4 * QROWS), 1)))
    cut = one_hot(grid_row(iota((4 * QROWS, 1), 0)) == iota((4 * QROWS, PADDED), 1))
    for copy, held, quads in ((t_copy, tok_v, xq), (c_copy, cot_v, cq)):
        copy.wait()
        raw[:, 0:4, :] = held[...]
        grid = raw[...].reshape(PADDED, D)
        quads[...] = nn(cut, grid).astype(BF).reshape(4, QROWS, D)
    pl.semaphore_wait(barrier, len(partners))

    def send(src, dst, ssem, rsem, where):
        copy = pltpu.make_async_remote_copy(
            src_ref=src, dst_ref=dst, send_sem=ssem, recv_sem=rsem,
            device_id=where, device_id_type=MESH,
        )
        copy.start()
        return copy

    halo_x = [send(xq.at[q], hx.at[q - 1], hs.at[q - 1], hr.at[q - 1], back[q]) for q in (3, 1, 2)]
    halo_c = [send(cq.at[q], hc.at[q - 1], hs.at[q + 2], hr.at[q + 2], back[q]) for q in (3, 1, 2)]

    s_col = iota((2 * WIN, 1), 0)
    sel[...] = one_hot(iota((2 * WIN, 4 * QROWS), 1) == quad_row(s_col))
    for w in range(2):
        s_row = iota((1, WIN), 1) + w * WIN
        selt[w] = one_hot(iota((4 * QROWS, WIN), 0) == quad_row(s_row))
    r = iota((D, 1), 0)
    half = r >> 8
    a = r & 255
    is_a = a < 128
    is_b = a < 192
    b = a & 63
    f_x = jnp.where(is_a, a >> 5, jnp.where(is_b, b >> 4, (b >> 3) & 3))
    f_zh = jnp.where(is_a, (a >> 4) & 1, jnp.where(is_b, (b >> 3) & 1, b >> 5))
    f_i = jnp.where(is_a, a & 15, jnp.where(is_b, 16 + (b & 7), 24 + (b & 7)))
    f_c = jnp.where(half == 0, 1 - core, core)
    perm[...] = one_hot(iota((D, D), 1) == f_zh * 256 + f_x * 64 + f_c * 32 + f_i)
    r_q[...] = jnp.zeros_like(r_q)
    r_o[...] = jnp.zeros_like(r_o)

    quad, _, row, col = token_place(iota((WIN, 1), 0))
    l_row = lat * 6 + 3 + (quad & 1) * 3 + row
    l_row = jnp.where(l_row >= 96, l_row - 96, l_row)
    l_col = lon * 12 + 6 + (quad >> 1) * 6 + col
    l_col = jnp.where(l_col >= 384, l_col - 384, l_col)
    picked = nn(one_hot(iota((WIN, 96), 1) == l_row), land[...].astype(F32).astype(BF))
    land_key = jnp.sum(jnp.where(iota((WIN, 384), 1) == l_col, picked, 0.0), axis=1, keepdims=True)

    def region(t, w):
        quad, lev, _, _ = token_place(t)
        seam = jnp.where(lat == 15, 2, 0)
        return seam * (quad & 1) + (lev if w == 1 else 0)

    masks = [
        jnp.where(region(iota((WIN, 1), 0), w) == region(iota((1, WIN), 1), w), 0.0, -1e30)
        for w in range(2)
    ]

    w_copy.wait()
    o_copy.wait()
    eye = one_hot(iota((256, 256), 0) == iota((256, 256), 1))
    for k in range(6):
        wt[256 * k : 256 * k + 256] = nt(eye, wqkv[:, 256 * k : 256 * k + 256]).astype(BF)

    def layer_norm(x, q):
        x = x.astype(F32)
        centred = x - jnp.mean(x, axis=1, keepdims=True)
        scale = lax.rsqrt(jnp.mean(centred * centred, axis=1, keepdims=True) + 1e-05)
        normal[q] = centred * scale
        inv[q] = jnp.broadcast_to(scale, (QROWS, 128))

    layer_norm(xq[0], 0)
    for copy, q in zip(halo_x, (3, 1, 2)):
        copy.wait()
        layer_norm(hx[q - 1], q)
    normed = normal[...].reshape(4 * QROWS, D).astype(BF)
    normw[...] = nn(sel[...], normed).astype(BF)
    for w in range(2):
        nw = normw[WIN * w : WIN * w + WIN]
        qkvt[w] = nt(wt[...], nw).astype(BF)
        nmt[w] = nt(perm[...], nw).astype(BF)
    for copy in halo_c:
        copy.wait()
    cot = jnp.concatenate([cq[0], hc[0], hc[1], hc[2]], axis=0)
    cotw[...] = nn(sel[...], cot).astype(BF)
    for w in range(2):
        cw = cotw[WIN * w : WIN * w + WIN]
        dmt[w] = nt(wout[...], cw).astype(BF)
        for k in range(2):
            ct = nt(eye, cw[:, 256 * k : 256 * k + 256]).astype(BF)
            for g in range(16):
                at = 64 * (16 * k + g) + 48
                r_o[w, at : at + 16] = ct[16 * g : 16 * g + 16]

    def one_head(h):
        base = h * HD
        bias_h = bias[h]
        d_bias = jnp.zeros((1, WIN), F32)
        for w in range(2):
            qt = qkvt[w, pl.ds(base, HD)]
            kt = qkvt[w, pl.ds(D + base, HD)]
            vt = qkvt[w, pl.ds(2 * D + base, HD)]
            dm = dmt[w, pl.ds(base, HD)]
            score = tn(kt, qt) * (HD ** -0.5) + (bias_h * land_key + masks[w])
            expo = jnp.exp(score - jnp.max(score, axis=0, keepdims=True))
            prob = expo * (1.0 / jnp.sum(expo, axis=0, keepdims=True))
            prob_b = prob.astype(BF)
            mixt[w, pl.ds(base, HD)] = nn(vt, prob_b).astype(BF)
            d_prob = tn(vt, dm).astype(BF).astype(F32)
            d_v = nt(dm, prob_b).astype(BF)
            d_score = prob * (d_prob - jnp.sum(prob * d_prob, axis=0, keepdims=True))
            d_bias = d_bias + jnp.sum(d_score * land_key, axis=0, keepdims=True)
            ds_b = d_score.astype(BF)
            d_q = (nn(kt, ds_b) * (HD ** -0.5)).astype(BF)
            d_k = (nt(qt, ds_b) * (HD ** -0.5)).astype(BF)
            for part, grad in enumerate((d_q, d_k, d_v)):
                dqkvt[w, pl.ds(part * D + base, HD)] = grad
                for g in range(4):
                    piece = h * 4 + (part * 32 + g)
                    at = (piece // 3) * 64 + (piece % 3) * 16
                    r_q[w, pl.ds(at, 16)] = grad[16 * g : 16 * g + 16]
        dbias[h : h + 1] = d_bias

    for h in range(HEADS):
        one_head(h)

    bc[0] = jnp.broadcast_to(jnp.sum(dbias[...], axis=1, keepdims=True), (HEADS, 128))
    bias_c = send(bc.at[0], bc.at[1], cs.at[0], cr.at[0], at_core())

    for w in range(2):
        mixp[w] = nn(perm[...], mixt[w]).astype(BF)

    def grad_block(first, y):
        cols = slice(y * 256, y * 256 + 256)
        total = None
        for w in range(2):
            for left, right in ((nmt, r_q), (mixp, r_o)):
                term = nt(left[w, first : first + 256], right[w, cols])
                total = term if total is None else total + term
        return total

    core_copies = []
    for y in range(NY):
        core_s[y] = grad_block(0, y).astype(BF)
        if y % 2 == 1:
            pair, k = slice(y - 1, y + 1), 1 + y // 2
            core_copies.append(send(core_s.at[pair], core_r.at[pair], cs.at[k], cr.at[k], at_core()))

    out_sends = []

    def give(q, value, mine, away, far, k):
        if q == 0:
            mine[0] = value
        else:
            away[q - 1] = value
            out_sends.append(send(away.at[q - 1], far.at[q], os.at[k], orr.at[k], ahead[q]))

    for q in (3, 1, 2, 0):
        rows = slice(QROWS * q, QROWS * q + QROWS)
        mixed = (nt(selt[0, rows], mixt[0]) + nt(selt[1, rows], mixt[1])).astype(BF)
        give(q, nn(mixed, wout[...]).astype(BF), att_q, oa, att_q, q - 1)

    lane_low = iota((64, 128), 1) < 64
    kept = []
    for y in range(NY):
        if y % 2 == 0:
            core_copies[y // 2].wait()
        total = grad_block(256, y) + core_r[y].astype(F32)
        for x in range(NX):
            a1[x, y] = total[32 * x : 32 * x + 32].astype(BF)
        b1[y] = total[128:192].astype(BF)
        kept.append(total[192:256])
        if y % 2 == 1:
            m = y // 2
            for t in range(2):
                lo = kept[0][:, 128 * t : 128 * t + 128]
                hi = kept[1][:, 128 * t : 128 * t + 128]
                even = jnp.where(lane_low, lo, pltpu.roll(hi, 64, 1)).astype(BF)
                odd = jnp.where(lane_low, pltpu.roll(lo, 64, 1), hi).astype(BF)
                for zh in range(2):
                    c1[zh * 4 + 2 * t, :, 128 * m : 128 * m + 128] = even[32 * zh : 32 * zh + 32]
                    c1[zh * 4 + 2 * t + 1, :, 128 * m : 128 * m + 128] = odd[32 * zh : 32 * zh + 32]
            kept = []

    def swap_x(src, dst, stage):
        return [send(src(d), dst.at[d - 1], xs.at[stage, d - 1], xr.at[stage, d - 1], at_x(d)) for d in (2, 1, 3)]

    def swap_y(src, dst, stage):
        return [send(src(d), dst.at[d - 1], ys.at[stage, d - 1], yr.at[stage, d - 1], at_y(d)) for d in (4, 3, 5, 2, 6, 1, 7)]

    def swap_z(src, dst, stage):
        return [send(src(d), dst.at[d - 1], zs.at[stage, d - 1], zr.at[stage, d - 1], at_z(d)) for d in (4, 3, 5, 2, 6, 1, 7)]

    def wait(copies):
        for copy in copies:
            copy.wait()

    def summed(own_part, parts, count):
        total = own_part.astype(F32)
        for d in range(count):
            total = total + parts[d].astype(F32)
        return total

    go_c = swap_z(lambda d: c1.at[(pz + d) & 7], rc1, 0)
    go_b = swap_y(lambda d: b1.at[(py + d) & 7], rb1, 0)
    go_a = swap_x(lambda d: a1.at[(px + d) & 3], ra1, 0)
    bias_c.wait()
    bx[0] = bc[0] + bc[1]
    go_bias = [send(bx.at[0], bx.at[d], xs.at[3, d - 1], xr.at[3, d - 1], at_x(d)) for d in (2, 1, 3)]

    for q in (3, 1, 2, 0):
        rows = slice(QROWS * q, QROWS * q + QROWS)
        d_qkv = (nt(selt[0, rows], dqkvt[0]) + nt(selt[1, rows], dqkvt[1])).astype(BF)
        d_normed = nn(d_qkv, wt[...])
        norm = normal[q]
        mean_grad = jnp.mean(d_normed, axis=1, keepdims=True)
        mean_cross = jnp.mean(d_normed * norm, axis=1, keepdims=True)
        d_tok = (inv[q][:, 0:1] * (d_normed - mean_grad - norm * mean_cross)).astype(BF)
        give(q, d_tok, tok_q, ot, tok_q, q + 2)

    wait(go_a)
    for y in range(NY):
        total = a1[px, y].astype(F32)
        for d in range(3):
            total = total + ra1[d, y].astype(F32)
        a2[y] = total.astype(BF)
    go_a = swap_y(lambda d: a2.at[(py + d) & 7], ra2, 1)
    wait(go_b)
    total = summed(b1[py], rb1, 7)
    for zh in range(2):
        for t in range(2):
            for x in range(NX):
                at = 16 * x + 8 * zh
                b2[zh * 2 + t, 8 * x : 8 * x + 8] = total[at : at + 8, 128 * t : 128 * t + 128]
    go_b = swap_z(lambda d: b2.at[((pz + d) & 7) >> 1], rb2, 1)
    wait(go_c)
    total = summed(c1[pz], rc1, 7)
    for x in range(NX):
        c2[x] = total[8 * x : 8 * x + 8]
    go_c = swap_x(lambda d: c2.at[(px + d) & 3], rc2, 1)
    wait(go_bias)

    def ordered(slots, me, n):
        total = slots[me & (n - 1)]
        for k in range(1, n):
            total = total + slots[(me - k) & (n - 1)]
        return total

    by[0] = ordered(bx, px, NX)
    go_bias = [send(by.at[0], by.at[d], ys.at[3, d - 1], yr.at[3, d - 1], at_y(d)) for d in (4, 3, 5, 2, 6, 1, 7)]

    wait(go_a)
    total = summed(a2[py], ra2, 7)
    for zh in range(2):
        for t in range(2):
            a3[zh * 2 + t] = total[16 * zh : 16 * zh + 16, 128 * t : 128 * t + 128]
    go_a = swap_z(lambda d: a3.at[((pz + d) & 7) >> 1], ra3, 2)
    wait(go_b)
    total = summed(b2[pz >> 1], rb2, 7)
    for x in range(NX):
        b3[x] = total[8 * x : 8 * x + 8]
    go_b = swap_x(lambda d: b3.at[(px + d) & 3], rb3, 2)
    wait(go_c)
    total = summed(c2[px], rc2, 3)
    for m in range(4):
        c3[m] = total[:, 128 * m : 128 * m + 128]
    go_c = swap_y(lambda d: c3.at[((py + d) & 7) >> 1], rc3, 2)
    wait(go_bias)
    bz[0] = ordered(by, py, NY)
    go_bias = [send(bz.at[0], bz.at[d], zs.at[3, d - 1], zr.at[3, d - 1], at_z(d)) for d in (4, 3, 5, 2, 6, 1, 7)]

    def mine(total, odd):
        return jnp.where(odd == 1, pltpu.roll(total, 64, 1), total)

    wait(out_sends)
    for quads, out in ((att_q, out_att), (tok_q, out_tok)):
        grid = nn(spread[...], quads[...].reshape(4 * QROWS, D)).astype(BF)
        out[...] = grid.reshape(CELLS, 16, D)[:, 0:4, :]

    wait(go_a)
    grad_a = mine(summed(a3[pz >> 1], ra3, 7), pzl & 1)
    wait(go_b)
    grad_b = mine(summed(b3[px], rb3, 3), pzl & 1)
    wait(go_c)
    grad_c = mine(summed(c3[py >> 1], rc3, 7), py & 1)
    grads = jnp.concatenate([grad_a, grad_b, grad_c], axis=0)
    g_qkv[...] = grads[:, 0:48]
    g_out[...] = grads.T[48:64]
    wait(go_bias)
    total = ordered(bz, pz, NZ)
    on_diagonal = iota((HEADS, 128), 0) == iota((HEADS, 128), 1)
    g_bias[...] = jnp.sum(jnp.where(on_diagonal, total, 0.0), axis=0, keepdims=True)[:, 0:HEADS]


def place(*refs):
    count = len(refs) // 2
    for k in range(count):
        refs[count + k][...] = refs[k][...]


def cells(grid):
    return grid.transpose(1, 2, 0, 3).reshape(CELLS, 4, D)


def levels(grid):
    return grid.reshape(6, 12, 4, D).transpose(2, 0, 1, 3)


def shards(tokens, cotangent, w_qkv, w_out, land_mask, land_bias):
    vmem = pl.BlockSpec(memory_space=pltpu.VMEM)
    anywhere = pl.BlockSpec(memory_space=pl.ANY)
    V = pltpu.VMEM
    dma = pltpu.SemaphoreType.DMA
    att, tok, g_qkv, g_out, g_bias = pl.pallas_call(
        kernel,
        out_shape=[
            jax.ShapeDtypeStruct((CELLS, 4, D), BF),
            jax.ShapeDtypeStruct((CELLS, 4, D), BF),
            jax.ShapeDtypeStruct((32, 48), F32),
            jax.ShapeDtypeStruct((16, 32), F32),
            jax.ShapeDtypeStruct((1, HEADS), F32),
        ],
        in_specs=[anywhere, anywhere, anywhere, anywhere, vmem, pl.BlockSpec(memory_space=pltpu.SMEM)],
        out_specs=[vmem] * 5,
        scratch_shapes=[
            V((CELLS, 4, D), BF), V((CELLS, 4, D), BF), V((CELLS, 16, D), BF),
            V((4, QROWS, D), BF), V((4, QROWS, D), BF),
            V((3, QROWS, D), BF), V((3, QROWS, D), BF),
            V((4, QROWS, D), BF), V((4, QROWS, D), BF), V((PADDED, 4 * QROWS), BF),
            V((D, 3 * D), BF), V((D, D), BF), V((3 * D, D), BF),
            V((D, D), BF), V((2 * WIN, 4 * QROWS), BF), V((2, 4 * QROWS, WIN), BF),
            V((4, QROWS, D), F32), V((4, QROWS, 128), F32),
            V((2 * WIN, D), BF), V((2 * WIN, D), BF),
            V((2, D, WIN), BF), V((2, 3 * D, WIN), BF), V((2, D, WIN), BF),
            V((2, D, WIN), BF), V((2, D, WIN), BF), V((2, 3 * D, WIN), BF),
            V((2, 4 * D, WIN), BF), V((2, 4 * D, WIN), BF),
            V((3, QROWS, D), BF), V((3, QROWS, D), BF),
            V((NY, 256, 256), BF), V((NY, 256, 256), BF),
            V((NX, NY, 32, 256), BF), V((3, NY, 32, 256), BF),
            V((NY, 32, 256), BF), V((7, 32, 256), BF),
            V((4, 16, 128), F32), V((7, 16, 128), F32),
            V((NY, 64, 256), BF), V((7, 64, 256), BF),
            V((4, 32, 128), F32), V((7, 32, 128), F32),
            V((NX, 8, 128), F32), V((3, 8, 128), F32),
            V((NZ, 32, 512), BF), V((7, 32, 512), BF),
            V((NX, 8, 512), F32), V((3, 8, 512), F32),
            V((4, 8, 128), F32), V((7, 8, 128), F32),
            V((HEADS, WIN), F32), V((2, HEADS, 128), F32),
            V((NX, HEADS, 128), F32), V((NY, HEADS, 128), F32), V((NZ, HEADS, 128), F32),
            dma((4,)), dma((6,)), dma((6,)), dma((6,)), dma((6,)),
            dma((5,)), dma((5,)),
            dma((4, 3)), dma((4, 3)), dma((4, 7)), dma((4, 7)), dma((4, 7)), dma((4, 7)),
        ],
        compiler_params=pltpu.CompilerParams(
            collective_id=0, has_side_effects=True, vmem_limit_bytes=60 << 20
        ),
        name="swin_block",
    )(cells(tokens), cells(cotangent), w_qkv, w_out, land_mask, land_bias)
    results = (att, tok, g_qkv, g_out, g_bias)
    att, tok, g_qkv, g_out, g_bias = pl.pallas_call(
        place,
        out_shape=[jax.ShapeDtypeStruct(x.shape, x.dtype) for x in results],
        in_specs=[vmem] * 5,
        out_specs=[vmem] * 5,
        compiler_params=pltpu.CompilerParams(vmem_limit_bytes=60 << 20),
        name="place",
    )(*results)
    return levels(att), levels(tok), g_qkv, g_out.T, g_bias.reshape(HEADS)


def solution(mesh):
    in_specs = (P(None, "lat", "lon", None), P(None, "lat", "lon", None), P(), P(), P(), P())
    out_specs = (
        P(None, "lat", "lon", None),
        P(None, "lat", "lon", None),
        P("lat", "lon"),
        P("lat", "lon"),
        P(),
    )
    return jax.shard_map(shards, mesh=mesh, in_specs=in_specs, out_specs=out_specs, check_vma=False)
```

```python
import jax
import jax.numpy as jnp
from jax import lax
from jax.experimental import pallas as pl
from jax.experimental.pallas import tpu as pltpu
from jax.sharding import PartitionSpec as P

MESH = pl.DeviceIdType.MESH
BF = jnp.bfloat16
F32 = jnp.float32
D = 512
HEADS = 8
HD = 64
WIN = 144
PART = 36
CELLS = 72
PADDED = CELLS * 8
QROWS = 80
NX, NY, NZ = 4, 8, 8


def nn(a, b):
    return lax.dot_general(a, b, (((1,), (0,)), ((), ())), preferred_element_type=F32)


def nt(a, b):
    return lax.dot_general(a, b, (((1,), (1,)), ((), ())), preferred_element_type=F32)


def tn(a, b):
    return lax.dot_general(a, b, (((0,), (0,)), ((), ())), preferred_element_type=F32)


def iota(shape, axis):
    return lax.broadcasted_iota(jnp.int32, shape, axis)


def one_hot(cond):
    return jnp.where(cond, 1.0, 0.0).astype(BF)


def token_place(t):
    quad = (t >= 36).astype(jnp.int32) + (t >= 72).astype(jnp.int32) + (t >= 108).astype(jnp.int32)
    rem = t - 36 * quad
    lev = (rem >= 18).astype(jnp.int32)
    pos = rem - 18 * lev
    row = (pos >= 6).astype(jnp.int32) + (pos >= 12).astype(jnp.int32)
    return quad, lev, row, pos - 6 * row


def quad_row(s):
    w = (s >= WIN).astype(jnp.int32)
    t = s - WIN * w
    quad = (t >= 36).astype(jnp.int32) + (t >= 72).astype(jnp.int32) + (t >= 108).astype(jnp.int32)
    return quad * QROWS + w * PART + (t - 36 * quad)


def grid_row(s):
    quad = (s >= QROWS).astype(jnp.int32) + (s >= 2 * QROWS).astype(jnp.int32) + (s >= 3 * QROWS).astype(jnp.int32)
    rem = s - QROWS * quad
    step = (rem >= 18).astype(jnp.int32) + (rem >= 36).astype(jnp.int32) + (rem >= 54).astype(jnp.int32)
    pos = rem - 18 * step
    row = (pos >= 6).astype(jnp.int32) + (pos >= 12).astype(jnp.int32)
    col = pos - 6 * row
    lev = (step + 1) & 3
    at = ((3 * (1 - (quad & 1)) + row) * 12 + 6 * (1 - (quad >> 1)) + col) * 8 + lev
    return jnp.where(rem < 72, at, -1)


def kernel(
    tok_h, cot_h, wqkv_h, wout_h, land, bias,
    out_att, out_tok, g_qkv, g_out, g_bias,
    tok_v, cot_v, raw, xq, cq, hx, hc, att_q, tok_q, spread, probs, prob_b, d_prob, d_score, ka, qa,
    wqkv, wout, wt, perm, sel, selt, normal, inv,
    normw, cotw, nmt, vt, dmt, mixt, mixp, dqkvt, r_q, r_o,
    oa, ot, core_s, core_r,
    a1, ra1, a2, ra2, a3, ra3, b1, rb1, b2, rb2, b3, rb3, c1, rc1, c2, rc2, c3, rc3,
    dbias, bc, bx, by, bz,
    lsem, hs, hr, os, orr, cs, cr, xs, xr, ys, yr, zs, zr,
):
    lat = lax.axis_index("lat")
    lon = lax.axis_index("lon")
    core = lat & 1
    px = (lat >> 1) & 3
    pzh = lat >> 3
    py = lon >> 2
    pzl = lon & 3
    pz = pzh * 4 + pzl

    def dev(x, y, z, c):
        return ((z >> 2) * 8 + x * 2 + c, y * 4 + (z & 3))

    def at_core():
        return dev(px, py, pz, 1 - core)

    def at_x(d):
        return dev((px + d) & 3, py, pz, core)

    def at_y(d):
        return dev(px, (py + d) & 7, pz, core)

    def at_z(d):
        return dev(px, py, (pz + d) & 7, core)

    back = [None, ((lat + 15) & 15, lon), (lat, (lon + 31) & 31), ((lat + 15) & 15, (lon + 31) & 31)]
    ahead = [None, ((lat + 1) & 15, lon), (lat, (lon + 1) & 31), ((lat + 1) & 15, (lon + 1) & 31)]

    barrier = pltpu.get_barrier_semaphore()
    partners = back[1:] + ahead[1:] + [at_core()]
    partners += [at_x(d) for d in range(1, NX)]
    partners += [at_y(d) for d in range(1, NY)] + [at_z(d) for d in range(1, NZ)]
    for where in partners:
        pl.semaphore_signal(barrier, inc=1, device_id=where, device_id_type=MESH)

    t_copy = pltpu.make_async_copy(tok_h, tok_v, lsem.at[2])
    t_copy.start()
    c_copy = pltpu.make_async_copy(cot_h, cot_v, lsem.at[3])
    c_copy.start()
    w_copy = pltpu.make_async_copy(wqkv_h, wqkv, lsem.at[0])
    w_copy.start()
    o_copy = pltpu.make_async_copy(wout_h, wout, lsem.at[1])
    o_copy.start()
    raw[...] = jnp.zeros_like(raw)
    cut = one_hot(grid_row(iota((4 * QROWS, 1), 0)) == iota((4 * QROWS, PADDED), 1))

    def cut_up(copy, held, quads):
        copy.wait()
        raw[:, 0:4, :] = held[...].astype(F32)
        grid = raw[...].reshape(PADDED, D).astype(BF)
        quads[...] = nn(cut, grid).astype(BF).reshape(4, QROWS, D)

    cut_up(t_copy, tok_v, xq)
    pl.semaphore_wait(barrier, len(partners))

    def send(src, dst, ssem, rsem, where):
        copy = pltpu.make_async_remote_copy(
            src_ref=src, dst_ref=dst, send_sem=ssem, recv_sem=rsem,
            device_id=where, device_id_type=MESH,
        )
        copy.start()
        return copy

    halo_x = [send(xq.at[q], hx.at[q - 1], hs.at[q - 1], hr.at[q - 1], back[q]) for q in (3, 1, 2)]
    cut_up(c_copy, cot_v, cq)

    spread[...] = one_hot(iota((PADDED, 4 * QROWS), 0) == grid_row(iota((1, 4 * QROWS), 1)))
    s_col = iota((2 * WIN, 1), 0)
    sel[...] = one_hot(iota((2 * WIN, 4 * QROWS), 1) == quad_row(s_col))
    for w in range(2):
        s_row = iota((1, WIN), 1) + w * WIN
        selt[w] = one_hot(iota((4 * QROWS, WIN), 0) == quad_row(s_row))
    r = iota((D, 1), 0)
    half = r >> 8
    a = r & 255
    is_a = a < 128
    is_b = a < 192
    b = a & 63
    f_x = jnp.where(is_a, a >> 5, jnp.where(is_b, b >> 4, (b >> 3) & 3))
    f_zh = jnp.where(is_a, (a >> 4) & 1, jnp.where(is_b, (b >> 3) & 1, b >> 5))
    f_i = jnp.where(is_a, a & 15, jnp.where(is_b, 16 + (b & 7), 24 + (b & 7)))
    f_c = jnp.where(half == 0, 1 - core, core)
    perm[...] = one_hot(iota((D, D), 1) == f_zh * 256 + f_x * 64 + f_c * 32 + f_i)

    for copy in halo_x:
        copy.wait_send()
    halo_c = [send(cq.at[q], hc.at[q - 1], hs.at[q + 2], hr.at[q + 2], back[q]) for q in (3, 1, 2)]
    r_q[...] = jnp.zeros_like(r_q)
    r_o[...] = jnp.zeros_like(r_o)

    quad, _, row, col = token_place(iota((1, WIN), 1))
    l_row = lat * 6 + 3 + (quad & 1) * 3 + row
    l_row = jnp.where(l_row >= 96, l_row - 96, l_row)
    l_col = lon * 12 + 6 + (quad >> 1) * 6 + col
    l_col = jnp.where(l_col >= 384, l_col - 384, l_col)
    picked = nn(land[...].astype(F32).astype(BF), one_hot(iota((384, WIN), 0) == l_col))
    land_key = jnp.sum(jnp.where(iota((96, WIN), 0) == l_row, picked, 0.0), axis=0, keepdims=True)

    extra = iota((16, WIN), 0)
    is_land = (extra >= 4) & (extra < 7)
    for w in range(2):
        quad, lev, _, _ = token_place(iota((16, WIN), 1))
        region = jnp.where(lat == 15, 2, 0) * (quad & 1) + (lev if w == 1 else 0)
        here = extra == region
        under_keys = jnp.where(here, 1.0, jnp.where(is_land, land_key, 0.0)).astype(BF)
        barred = jnp.where(here | (extra >= 4), 0.0, -1e30)
        for h in range(HEADS):
            full = jnp.zeros((16, WIN), F32) + bias[h]
            first = full.astype(BF).astype(F32)
            second = (full - first).astype(BF).astype(F32)
            third = full - first - second
            pieces = jnp.where(extra == 4, first, jnp.where(extra == 5, second, third))
            ka[w, h, HD : HD + 16] = under_keys
            qa[w, h, HD : HD + 16] = jnp.where(is_land, pieces, barred).astype(BF)

    w_copy.wait()
    o_copy.wait()
    eye = one_hot(iota((256, 256), 0) == iota((256, 256), 1))
    for k in range(6):
        wt[256 * k : 256 * k + 256] = nt(eye, wqkv[:, 256 * k : 256 * k + 256]).astype(BF)

    def layer_norm(x, q):
        x = x.astype(F32)
        centred = x - jnp.mean(x, axis=1, keepdims=True)
        scale = lax.rsqrt(jnp.mean(centred * centred, axis=1, keepdims=True) + 1e-05)
        normal[q] = centred * scale
        inv[q] = jnp.broadcast_to(scale, (QROWS, 128))

    layer_norm(xq[0], 0)
    for copy, q in zip(halo_x, (3, 1, 2)):
        copy.wait_recv()
        layer_norm(hx[q - 1], q)
    normed = normal[...].reshape(4 * QROWS, D).astype(BF)
    normw[...] = nn(sel[...], normed).astype(BF)
    for w in range(2):
        nw = normw[WIN * w : WIN * w + WIN]
        qkv = nt(wt[...], nw).astype(BF)
        for h in range(HEADS):
            qa[w, h, 0:HD] = qkv[h * HD : h * HD + HD] * (HD ** -0.5)
            ka[w, h, 0:HD] = qkv[D + h * HD : D + h * HD + HD]
        vt[w] = qkv[2 * D :]
        nmt[w] = nt(perm[...], nw).astype(BF)
    pairs = [(w, h) for h in range(HEADS) for w in range(2)]

    def head(h):
        return slice(h * HD, h * HD + HD)

    for w, h in pairs:
        probs[w, h] = tn(ka[w, h], qa[w, h])
    for w, h in pairs:
        score = probs[w, h]
        expo = jnp.exp(score - jnp.max(score, axis=0, keepdims=True))
        prob = expo * (1.0 / jnp.sum(expo, axis=0, keepdims=True))
        probs[w, h] = prob
        prob_b[w, h] = prob.astype(BF)
    for w, h in pairs:
        mixt[w, head(h)] = nn(vt[w, head(h)], prob_b[w, h]).astype(BF)

    out_sends = []

    def give(q, value, mine, away, far, k):
        if q == 0:
            mine[0] = value
        else:
            away[q - 1] = value
            out_sends.append(send(away.at[q - 1], far.at[q], os.at[k], orr.at[k], ahead[q]))

    for q in (3, 1, 2, 0):
        rows = slice(QROWS * q, QROWS * q + QROWS)
        mixed = (nt(selt[0, rows], mixt[0]) + nt(selt[1, rows], mixt[1])).astype(BF)
        give(q, nn(mixed, wout[...]).astype(BF), att_q, oa, att_q, q - 1)

    for copy in halo_c:
        copy.wait()
    cot = jnp.concatenate([cq[0], hc[0], hc[1], hc[2]], axis=0)
    cotw[...] = nn(sel[...], cot).astype(BF)
    for w in range(2):
        cw = cotw[WIN * w : WIN * w + WIN]
        dmt[w] = nt(wout[...], cw).astype(BF)
        for k in range(2):
            ct = nt(eye, cw[:, 256 * k : 256 * k + 256]).astype(BF)
            for g in range(16):
                at = 64 * (16 * k + g) + 48
                r_o[w, at : at + 16] = ct[16 * g : 16 * g + 16]

    for w, h in pairs:
        d_prob[w, h] = tn(vt[w, head(h)], dmt[w, head(h)]).astype(BF)

    def keep(w, h, k, grad):
        dqkvt[w, k * D + h * HD : k * D + h * HD + HD] = grad
        for g in range(4):
            piece = h * 4 + k * 32 + g
            at = (piece // 3) * 64 + (piece % 3) * 16
            r_q[w, at : at + 16] = grad[16 * g : 16 * g + 16]

    for w, h in pairs:
        keep(w, h, 2, nt(dmt[w, head(h)], prob_b[w, h]).astype(BF))
    for w, h in pairs:
        prob = probs[w, h]
        dp = d_prob[w, h].astype(F32)
        d_score[w, h] = (prob * (dp - jnp.sum(prob * dp, axis=0, keepdims=True))).astype(BF)
    for w, h in pairs:
        under = nn(ka[w, h], d_score[w, h])
        keep(w, h, 0, (under[0:HD] * (HD ** -0.5)).astype(BF))
        dbias[w, h : h + 1] = under[HD + 4 : HD + 5]
        keep(w, h, 1, nt(qa[w, h, 0:HD], d_score[w, h]).astype(BF))

    bc[0] = jnp.broadcast_to(jnp.sum(dbias[0] + dbias[1], axis=1, keepdims=True), (HEADS, 128))
    bias_c = send(bc.at[0], bc.at[1], cs.at[0], cr.at[0], at_core())

    for w in range(2):
        mixp[w] = nn(perm[...], mixt[w]).astype(BF)

    def grad_block(first, y):
        cols = slice(y * 256, y * 256 + 256)
        total = None
        for w in range(2):
            for left, right in ((nmt, r_q), (mixp, r_o)):
                term = nt(left[w, first : first + 256], right[w, cols])
                total = term if total is None else total + term
        return total

    core_copies = []
    for y in range(NY):
        core_s[y] = grad_block(0, y).astype(BF)
        if y % 2 == 1:
            pair, k = slice(y - 1, y + 1), 1 + y // 2
            core_copies.append(send(core_s.at[pair], core_r.at[pair], cs.at[k], cr.at[k], at_core()))

    lane_low = iota((64, 128), 1) < 64
    kept = []
    for y in range(NY):
        if y % 2 == 0:
            core_copies[y // 2].wait()
        total = grad_block(256, y) + core_r[y].astype(F32)
        for x in range(NX):
            a1[x, y] = total[32 * x : 32 * x + 32].astype(BF)
        b1[y] = total[128:192].astype(BF)
        kept.append(total[192:256])
        if y % 2 == 1:
            m = y // 2
            for t in range(2):
                lo = kept[0][:, 128 * t : 128 * t + 128]
                hi = kept[1][:, 128 * t : 128 * t + 128]
                even = jnp.where(lane_low, lo, pltpu.roll(hi, 64, 1)).astype(BF)
                odd = jnp.where(lane_low, pltpu.roll(lo, 64, 1), hi).astype(BF)
                for zh in range(2):
                    c1[zh * 4 + 2 * t, :, 128 * m : 128 * m + 128] = even[32 * zh : 32 * zh + 32]
                    c1[zh * 4 + 2 * t + 1, :, 128 * m : 128 * m + 128] = odd[32 * zh : 32 * zh + 32]
            kept = []

    def swap_x(src, dst, stage):
        return [send(src(d), dst.at[d - 1], xs.at[stage, d - 1], xr.at[stage, d - 1], at_x(d)) for d in (2, 1, 3)]

    def swap_y(src, dst, stage):
        return [send(src(d), dst.at[d - 1], ys.at[stage, d - 1], yr.at[stage, d - 1], at_y(d)) for d in (4, 3, 5, 2, 6, 1, 7)]

    def swap_z(src, dst, stage):
        return [send(src(d), dst.at[d - 1], zs.at[stage, d - 1], zr.at[stage, d - 1], at_z(d)) for d in (4, 3, 5, 2, 6, 1, 7)]

    def wait(copies):
        for copy in copies:
            copy.wait()

    def summed(own_part, parts, count):
        total = own_part.astype(F32)
        for d in range(count):
            total = total + parts[d].astype(F32)
        return total

    go_a = swap_x(lambda d: a1.at[(px + d) & 3], ra1, 0)
    go_b = swap_y(lambda d: b1.at[(py + d) & 7], rb1, 0)
    go_c = swap_z(lambda d: c1.at[(pz + d) & 7], rc1, 0)
    bias_c.wait()
    bx[0] = bc[0] + bc[1]
    go_bias = [send(bx.at[0], bx.at[d], xs.at[3, d - 1], xr.at[3, d - 1], at_x(d)) for d in (2, 1, 3)]

    for q in (3, 1, 2, 0):
        rows = slice(QROWS * q, QROWS * q + QROWS)
        d_qkv = (nt(selt[0, rows], dqkvt[0]) + nt(selt[1, rows], dqkvt[1])).astype(BF)
        d_normed = nn(d_qkv, wt[...])
        norm = normal[q]
        mean_grad = jnp.mean(d_normed, axis=1, keepdims=True)
        mean_cross = jnp.mean(d_normed * norm, axis=1, keepdims=True)
        d_tok = (inv[q][:, 0:1] * (d_normed - mean_grad - norm * mean_cross)).astype(BF)
        give(q, d_tok, tok_q, ot, tok_q, q + 2)

    wait(go_a)
    for y in range(NY):
        total = a1[px, y].astype(F32)
        for d in range(3):
            total = total + ra1[d, y].astype(F32)
        a2[y] = total.astype(BF)
    go_a = swap_y(lambda d: a2.at[(py + d) & 7], ra2, 1)
    wait(go_b)
    total = summed(b1[py], rb1, 7)
    for zh in range(2):
        for t in range(2):
            for x in range(NX):
                at = 16 * x + 8 * zh
                b2[zh * 2 + t, 8 * x : 8 * x + 8] = total[at : at + 8, 128 * t : 128 * t + 128]
    go_b = swap_z(lambda d: b2.at[((pz + d) & 7) >> 1], rb2, 1)
    wait(go_c)
    total = summed(c1[pz], rc1, 7)
    for x in range(NX):
        c2[x] = total[8 * x : 8 * x + 8]
    go_c = swap_x(lambda d: c2.at[(px + d) & 3], rc2, 1)
    wait(go_bias)

    def ordered(slots, me, n):
        total = slots[me & (n - 1)]
        for k in range(1, n):
            total = total + slots[(me - k) & (n - 1)]
        return total

    by[0] = ordered(bx, px, NX)
    go_bias = [send(by.at[0], by.at[d], ys.at[3, d - 1], yr.at[3, d - 1], at_y(d)) for d in (4, 3, 5, 2, 6, 1, 7)]

    def to_grid(quads, out):
        grid = nn(spread[...], quads[...].reshape(4 * QROWS, D))
        out[...] = grid.reshape(CELLS, 8, D)[:, 0:4, :].astype(BF)

    wait(out_sends[:3])
    to_grid(att_q, out_att)

    wait(go_a)
    total = summed(a2[py], ra2, 7)
    for zh in range(2):
        for t in range(2):
            a3[zh * 2 + t] = total[16 * zh : 16 * zh + 16, 128 * t : 128 * t + 128]
    go_a = swap_z(lambda d: a3.at[((pz + d) & 7) >> 1], ra3, 2)
    wait(go_b)
    total = summed(b2[pz >> 1], rb2, 7)
    for x in range(NX):
        b3[x] = total[8 * x : 8 * x + 8]
    go_b = swap_x(lambda d: b3.at[(px + d) & 3], rb3, 2)
    wait(go_c)
    total = summed(c2[px], rc2, 3)
    for m in range(4):
        c3[m] = total[:, 128 * m : 128 * m + 128]
    go_c = swap_y(lambda d: c3.at[((py + d) & 7) >> 1], rc3, 2)
    wait(go_bias)
    bz[0] = ordered(by, py, NY)
    go_bias = [send(bz.at[0], bz.at[d], zs.at[3, d - 1], zr.at[3, d - 1], at_z(d)) for d in (4, 3, 5, 2, 6, 1, 7)]

    def mine(total, odd):
        return jnp.where(odd == 1, pltpu.roll(total, 64, 1), total)

    wait(out_sends[3:])
    to_grid(tok_q, out_tok)

    wait(go_a)
    grad_a = mine(summed(a3[pz >> 1], ra3, 7), pzl & 1)
    wait(go_b)
    grad_b = mine(summed(b3[px], rb3, 3), pzl & 1)
    wait(go_c)
    grad_c = mine(summed(c3[py >> 1], rc3, 7), py & 1)
    grads = jnp.concatenate([grad_a, grad_b, grad_c], axis=0)
    g_qkv[...] = grads[:, 0:48]
    g_out[...] = grads.T[48:64]
    wait(go_bias)
    total = ordered(bz, pz, NZ)
    on_diagonal = iota((HEADS, 128), 0) == iota((HEADS, 128), 1)
    g_bias[...] = jnp.sum(jnp.where(on_diagonal, total, 0.0), axis=0, keepdims=True)[:, 0:HEADS]


def place(*refs):
    count = (len(refs) - 2) // 3
    src, dst, held = refs[:count], refs[count : 2 * count], refs[2 * count : 3 * count]
    came, went = refs[-2:]
    into = [pltpu.make_async_copy(src[k], held[k], came.at[k]) for k in range(count)]
    out = [pltpu.make_async_copy(held[k], dst[k], went.at[k]) for k in range(count)]
    for copy in into:
        copy.start()
    for k in range(count):
        into[k].wait()
        out[k].start()
    for copy in out:
        copy.wait()


def cells(grid):
    return grid.transpose(1, 2, 0, 3).reshape(CELLS, 4, D)


def levels(grid):
    return grid.reshape(6, 12, 4, D).transpose(2, 0, 1, 3)


def shards(tokens, cotangent, w_qkv, w_out, land_mask, land_bias):
    vmem = pl.BlockSpec(memory_space=pltpu.VMEM)
    anywhere = pl.BlockSpec(memory_space=pl.ANY)
    V = pltpu.VMEM
    dma = pltpu.SemaphoreType.DMA
    att, tok, g_qkv, g_out, g_bias = pl.pallas_call(
        kernel,
        out_shape=[
            jax.ShapeDtypeStruct((CELLS, 4, D), BF),
            jax.ShapeDtypeStruct((CELLS, 4, D), BF),
            jax.ShapeDtypeStruct((32, 48), F32),
            jax.ShapeDtypeStruct((16, 32), F32),
            jax.ShapeDtypeStruct((1, HEADS), F32),
        ],
        in_specs=[anywhere, anywhere, anywhere, anywhere, vmem, pl.BlockSpec(memory_space=pltpu.SMEM)],
        out_specs=[vmem] * 5,
        scratch_shapes=[
            V((CELLS, 4, D), BF), V((CELLS, 4, D), BF), V((CELLS, 8, D), F32),
            V((4, QROWS, D), BF), V((4, QROWS, D), BF),
            V((3, QROWS, D), BF), V((3, QROWS, D), BF),
            V((4, QROWS, D), BF), V((4, QROWS, D), BF), V((PADDED, 4 * QROWS), BF),
            V((2, HEADS, WIN, WIN), F32), V((2, HEADS, WIN, WIN), BF),
            V((2, HEADS, WIN, WIN), BF), V((2, HEADS, WIN, WIN), BF),
            V((2, HEADS, HD + 16, WIN), BF), V((2, HEADS, HD + 16, WIN), BF),
            V((D, 3 * D), BF), V((D, D), BF), V((3 * D, D), BF),
            V((D, D), BF), V((2 * WIN, 4 * QROWS), BF), V((2, 4 * QROWS, WIN), BF),
            V((4, QROWS, D), F32), V((4, QROWS, 128), F32),
            V((2 * WIN, D), BF), V((2 * WIN, D), BF),
            V((2, D, WIN), BF), V((2, D, WIN), BF), V((2, D, WIN), BF),
            V((2, D, WIN), BF), V((2, D, WIN), BF), V((2, 3 * D, WIN), BF),
            V((2, 4 * D, WIN), BF), V((2, 4 * D, WIN), BF),
            V((3, QROWS, D), BF), V((3, QROWS, D), BF),
            V((NY, 256, 256), BF), V((NY, 256, 256), BF),
            V((NX, NY, 32, 256), BF), V((3, NY, 32, 256), BF),
            V((NY, 32, 256), BF), V((7, 32, 256), BF),
            V((4, 16, 128), F32), V((7, 16, 128), F32),
            V((NY, 64, 256), BF), V((7, 64, 256), BF),
            V((4, 32, 128), F32), V((7, 32, 128), F32),
            V((NX, 8, 128), F32), V((3, 8, 128), F32),
            V((NZ, 32, 512), BF), V((7, 32, 512), BF),
            V((NX, 8, 512), F32), V((3, 8, 512), F32),
            V((4, 8, 128), F32), V((7, 8, 128), F32),
            V((2, HEADS, WIN), F32), V((2, HEADS, 128), F32),
            V((NX, HEADS, 128), F32), V((NY, HEADS, 128), F32), V((NZ, HEADS, 128), F32),
            dma((4,)), dma((6,)), dma((6,)), dma((6,)), dma((6,)),
            dma((5,)), dma((5,)),
            dma((4, 3)), dma((4, 3)), dma((4, 7)), dma((4, 7)), dma((4, 7)), dma((4, 7)),
        ],
        compiler_params=pltpu.CompilerParams(
            collective_id=0, has_side_effects=True, vmem_limit_bytes=60 << 20
        ),
        name="swin_block",
    )(cells(tokens), cells(cotangent), w_qkv, w_out, land_mask, land_bias)
    results = (att, tok, g_qkv, g_out, g_bias)
    att, tok, g_qkv, g_out, g_bias = pl.pallas_call(
        place,
        out_shape=[jax.ShapeDtypeStruct(x.shape, x.dtype) for x in results],
        in_specs=[anywhere] * 5,
        out_specs=[anywhere] * 5,
        scratch_shapes=[V(x.shape, x.dtype) for x in results] + [dma((5,)), dma((5,))],
        compiler_params=pltpu.CompilerParams(vmem_limit_bytes=60 << 20),
        name="place",
    )(*results)
    return levels(att), levels(tok), g_qkv, g_out.T, g_bias.reshape(HEADS)


def solution(mesh):
    in_specs = (P(None, "lat", "lon", None), P(None, "lat", "lon", None), P(), P(), P(), P())
    out_specs = (
        P(None, "lat", "lon", None),
        P(None, "lat", "lon", None),
        P("lat", "lon"),
        P("lat", "lon"),
        P(),
    )
    return jax.shard_map(shards, mesh=mesh, in_specs=in_specs, out_specs=out_specs, check_vma=False)
```

```python
import jax
import jax.numpy as jnp
from jax import lax
from jax.experimental import pallas as pl
from jax.experimental.pallas import tpu as pltpu
from jax.sharding import PartitionSpec as P

MESH = pl.DeviceIdType.MESH
BF = jnp.bfloat16
F32 = jnp.float32
D = 512
HEADS = 8
HD = 64
WIN = 144
QROWS = 18 * 8
NX, NY, NZ = 4, 8, 8


def nn(a, b):
    return lax.dot_general(a, b, (((1,), (0,)), ((), ())), preferred_element_type=F32)


def nt(a, b):
    return lax.dot_general(a, b, (((1,), (1,)), ((), ())), preferred_element_type=F32)


def tn(a, b):
    return lax.dot_general(a, b, (((0,), (0,)), ((), ())), preferred_element_type=F32)


def iota(shape, axis):
    return lax.broadcasted_iota(jnp.int32, shape, axis)


def one_hot(cond):
    return jnp.where(cond, 1.0, 0.0).astype(BF)


def token_place(t):
    quad = (t >= 36).astype(jnp.int32) + (t >= 72).astype(jnp.int32) + (t >= 108).astype(jnp.int32)
    rem = t - 36 * quad
    lev = (rem >= 18).astype(jnp.int32)
    pos = rem - 18 * lev
    row = (pos >= 6).astype(jnp.int32) + (pos >= 12).astype(jnp.int32)
    return quad, lev, row, pos - 6 * row


def quad_row(s):
    w = (s >= WIN).astype(jnp.int32)
    quad, lev, row, col = token_place(s - WIN * w)
    return quad * QROWS + (row * 6 + col) * 8 + ((2 * w + lev + 1) & 3)


def kernel(
    tok_h, cot_h, wqkv_h, wout_h, land, bias,
    out_att, out_tok, g_qkv, g_out, g_bias,
    tok_v, cot_v, padded, hx, hc, probs, prob_b, d_prob, d_score, ka, qa,
    wqkv, wout, wt, perm, sel, selt, normal, inv,
    normw, cotw, nmt, vt, dmt, mixt, mixp, dqkvt, r_q, r_o,
    oa, ot, core_s, core_r,
    a1, ra1, a2, ra2, a3, ra3, b1, rb1, b2, rb2, b3, rb3, c1, rc1, c2, rc2, c3, rc3,
    dbias, bc, bx, by, bz,
    lsem, hs, hr, os, orr, cs, cr, xs, xr, ys, yr, zs, zr,
):
    lat = lax.axis_index("lat")
    lon = lax.axis_index("lon")
    core = lat & 1
    px = (lat >> 1) & 3
    pzh = lat >> 3
    py = lon >> 2
    pzl = lon & 3
    pz = pzh * 4 + pzl

    def dev(x, y, z, c):
        return ((z >> 2) * 8 + x * 2 + c, y * 4 + (z & 3))

    def at_core():
        return dev(px, py, pz, 1 - core)

    def at_x(d):
        return dev((px + d) & 3, py, pz, core)

    def at_y(d):
        return dev(px, (py + d) & 7, pz, core)

    def at_z(d):
        return dev(px, py, (pz + d) & 7, core)

    back = [None, ((lat + 15) & 15, lon), (lat, (lon + 31) & 31), ((lat + 15) & 15, (lon + 31) & 31)]
    ahead = [None, ((lat + 1) & 15, lon), (lat, (lon + 1) & 31), ((lat + 1) & 15, (lon + 1) & 31)]

    barrier = pltpu.get_barrier_semaphore()
    partners = back[1:] + ahead[1:] + [at_core()]
    partners += [at_x(d) for d in range(1, NX)]
    partners += [at_y(d) for d in range(1, NY)] + [at_z(d) for d in range(1, NZ)]
    for where in partners:
        pl.semaphore_signal(barrier, inc=1, device_id=where, device_id_type=MESH)

    t_copy = pltpu.make_async_copy(tok_h, tok_v, lsem.at[2])
    t_copy.start()
    c_copy = pltpu.make_async_copy(cot_h, cot_v, lsem.at[3])
    c_copy.start()
    w_copy = pltpu.make_async_copy(wqkv_h, wqkv, lsem.at[0])
    w_copy.start()
    o_copy = pltpu.make_async_copy(wout_h, wout, lsem.at[1])
    o_copy.start()
    t_copy.wait()
    c_copy.wait()
    pl.semaphore_wait(barrier, len(partners))

    def send(src, dst, ssem, rsem, where):
        copy = pltpu.make_async_remote_copy(
            src_ref=src, dst_ref=dst, send_sem=ssem, recv_sem=rsem,
            device_id=where, device_id_type=MESH,
        )
        copy.start()
        return copy

    places = [(slice(3 - 3 * (q & 1), 6 - 3 * (q & 1)), slice(6 - 6 * (q >> 1), 12 - 6 * (q >> 1))) for q in range(4)]

    def halo(held, far, first):
        return [
            send(held.at[places[q]], far.at[q - 1], hs.at[first + q - 1], hr.at[first + q - 1], back[q])
            for q in (3, 1, 2)
        ]

    halo_x = halo(tok_v, hx, 0)
    halo_c = halo(cot_v, hc, 3)

    padded[...] = jnp.zeros_like(padded)
    s_col = iota((2 * WIN, 1), 0)
    sel[...] = one_hot(iota((2 * WIN, 4 * QROWS), 1) == quad_row(s_col))
    for w in range(2):
        s_row = iota((1, WIN), 1) + w * WIN
        selt[w] = one_hot(iota((4 * QROWS, WIN), 0) == quad_row(s_row))
    r = iota((D, 1), 0)
    half = r >> 8
    a = r & 255
    is_a = a < 128
    is_b = a < 192
    b = a & 63
    f_x = jnp.where(is_a, a >> 5, jnp.where(is_b, b >> 4, (b >> 3) & 3))
    f_zh = jnp.where(is_a, (a >> 4) & 1, jnp.where(is_b, (b >> 3) & 1, b >> 5))
    f_i = jnp.where(is_a, a & 15, jnp.where(is_b, 16 + (b & 7), 24 + (b & 7)))
    f_c = jnp.where(half == 0, 1 - core, core)
    perm[...] = one_hot(iota((D, D), 1) == f_zh * 256 + f_x * 64 + f_c * 32 + f_i)

    r_q[...] = jnp.zeros_like(r_q)
    r_o[...] = jnp.zeros_like(r_o)

    quad, _, row, col = token_place(iota((1, WIN), 1))
    l_row = lat * 6 + 3 + (quad & 1) * 3 + row
    l_row = jnp.where(l_row >= 96, l_row - 96, l_row)
    l_col = lon * 12 + 6 + (quad >> 1) * 6 + col
    l_col = jnp.where(l_col >= 384, l_col - 384, l_col)
    picked = nn(land[...].astype(F32).astype(BF), one_hot(iota((384, WIN), 0) == l_col))
    land_key = jnp.sum(jnp.where(iota((96, WIN), 0) == l_row, picked, 0.0), axis=0, keepdims=True)

    extra = iota((16, WIN), 0)
    is_land = (extra >= 4) & (extra < 7)
    for w in range(2):
        quad, lev, _, _ = token_place(iota((16, WIN), 1))
        region = jnp.where(lat == 15, 2, 0) * (quad & 1) + (lev if w == 1 else 0)
        here = extra == region
        under_keys = jnp.where(here, 1.0, jnp.where(is_land, land_key, 0.0)).astype(BF)
        barred = jnp.where(here | (extra >= 4), 0.0, -1e30)
        for h in range(HEADS):
            full = jnp.zeros((16, WIN), F32) + bias[h]
            first = full.astype(BF).astype(F32)
            second = (full - first).astype(BF).astype(F32)
            third = full - first - second
            pieces = jnp.where(extra == 4, first, jnp.where(extra == 5, second, third))
            ka[w, h, HD : HD + 16] = under_keys
            qa[w, h, HD : HD + 16] = jnp.where(is_land, pieces, barred).astype(BF)

    w_copy.wait()
    o_copy.wait()
    eye = one_hot(iota((256, 256), 0) == iota((256, 256), 1))
    for k in range(6):
        wt[256 * k : 256 * k + 256] = nt(eye, wqkv[:, 256 * k : 256 * k + 256]).astype(BF)

    def gather(own, far, copies):
        padded[0, :, 0:4] = own[places[0]].reshape(18, 4, D).astype(F32)
        for copy, q in zip(copies, (3, 1, 2)):
            copy.wait()
            padded[q, :, 0:4] = far[q - 1].reshape(18, 4, D).astype(F32)
        return nn(sel[...], padded[...].reshape(4 * QROWS, D).astype(BF))

    x = gather(tok_v, hx, halo_x)
    centred = x - jnp.mean(x, axis=1, keepdims=True)
    scale = lax.rsqrt(jnp.mean(centred * centred, axis=1, keepdims=True) + 1e-05)
    normal[...] = centred * scale
    inv[...] = jnp.broadcast_to(scale, (2 * WIN, 128))
    normw[...] = normal[...].astype(BF)
    for w in range(2):
        nw = normw[WIN * w : WIN * w + WIN]
        qkv = nt(wt[...], nw).astype(BF)
        for h in range(HEADS):
            qa[w, h, 0:HD] = qkv[h * HD : h * HD + HD] * (HD ** -0.5)
            ka[w, h, 0:HD] = qkv[D + h * HD : D + h * HD + HD]
        vt[w] = qkv[2 * D :]
        nmt[w] = nt(perm[...], nw).astype(BF)
    pairs = [(w, h) for h in range(HEADS) for w in range(2)]

    def head(h):
        return slice(h * HD, h * HD + HD)

    for w, h in pairs:
        probs[w, h] = tn(ka[w, h], qa[w, h])
    for w, h in pairs:
        score = probs[w, h]
        expo = jnp.exp(score - jnp.max(score, axis=0, keepdims=True))
        prob = expo * (1.0 / jnp.sum(expo, axis=0, keepdims=True))
        probs[w, h] = prob
        prob_b[w, h] = prob.astype(BF)
    for w, h in pairs:
        mixt[w, head(h)] = nn(vt[w, head(h)], prob_b[w, h]).astype(BF)

    out_sends = []

    def give(q, value, away, far, k):
        value = value.reshape(18, 8, D)[:, 0:4].reshape(3, 6, 4, D).astype(BF)
        if q == 0:
            far[places[0]] = value
        else:
            away[q - 1] = value
            out_sends.append(send(away.at[q - 1], far.at[places[q]], os.at[k], orr.at[k], ahead[q]))

    for q in (3, 1, 2, 0):
        rows = slice(QROWS * q, QROWS * q + QROWS)
        mixed = (nt(selt[0, rows], mixt[0]) + nt(selt[1, rows], mixt[1])).astype(BF)
        give(q, nn(mixed, wout[...]), oa, out_att, q - 1)

    cotw[...] = gather(cot_v, hc, halo_c).astype(BF)
    for w in range(2):
        cw = cotw[WIN * w : WIN * w + WIN]
        dmt[w] = nt(wout[...], cw).astype(BF)
        for k in range(2):
            ct = nt(eye, cw[:, 256 * k : 256 * k + 256]).astype(BF)
            for g in range(16):
                at = 64 * (16 * k + g) + 48
                r_o[w, at : at + 16] = ct[16 * g : 16 * g + 16]

    for w, h in pairs:
        d_prob[w, h] = tn(vt[w, head(h)], dmt[w, head(h)]).astype(BF)

    def keep(w, h, k, grad):
        dqkvt[w, k * D + h * HD : k * D + h * HD + HD] = grad
        for g in range(4):
            piece = h * 4 + k * 32 + g
            at = (piece // 3) * 64 + (piece % 3) * 16
            r_q[w, at : at + 16] = grad[16 * g : 16 * g + 16]

    for w, h in pairs:
        keep(w, h, 2, nt(dmt[w, head(h)], prob_b[w, h]).astype(BF))
    for w, h in pairs:
        prob = probs[w, h]
        dp = d_prob[w, h].astype(F32)
        d_score[w, h] = (prob * (dp - jnp.sum(prob * dp, axis=0, keepdims=True))).astype(BF)
    for w, h in pairs:
        under = nn(ka[w, h], d_score[w, h])
        keep(w, h, 0, (under[0:HD] * (HD ** -0.5)).astype(BF))
        dbias[w, h : h + 1] = under[HD + 4 : HD + 5]
        keep(w, h, 1, nt(qa[w, h, 0:HD], d_score[w, h]).astype(BF))

    bc[0] = jnp.broadcast_to(jnp.sum(dbias[0] + dbias[1], axis=1, keepdims=True), (HEADS, 128))
    bias_c = send(bc.at[0], bc.at[1], cs.at[0], cr.at[0], at_core())

    for w in range(2):
        mixp[w] = nn(perm[...], mixt[w]).astype(BF)

    def grad_block(first, y):
        cols = slice(y * 256, y * 256 + 256)
        total = None
        for w in range(2):
            for left, right in ((nmt, r_q), (mixp, r_o)):
                term = nt(left[w, first : first + 256], right[w, cols])
                total = term if total is None else total + term
        return total

    core_copies = []
    for y in range(NY):
        core_s[y] = grad_block(0, y).astype(BF)
        if y % 2 == 1:
            pair, k = slice(y - 1, y + 1), 1 + y // 2
            core_copies.append(send(core_s.at[pair], core_r.at[pair], cs.at[k], cr.at[k], at_core()))

    lane_low = iota((64, 128), 1) < 64
    kept = []
    for y in range(NY):
        if y % 2 == 0:
            core_copies[y // 2].wait()
        total = grad_block(256, y) + core_r[y].astype(F32)
        for x in range(NX):
            a1[x, y] = total[32 * x : 32 * x + 32].astype(BF)
        b1[y] = total[128:192].astype(BF)
        kept.append(total[192:256])
        if y % 2 == 1:
            m = y // 2
            for t in range(2):
                lo = kept[0][:, 128 * t : 128 * t + 128]
                hi = kept[1][:, 128 * t : 128 * t + 128]
                even = jnp.where(lane_low, lo, pltpu.roll(hi, 64, 1)).astype(BF)
                odd = jnp.where(lane_low, pltpu.roll(lo, 64, 1), hi).astype(BF)
                for zh in range(2):
                    c1[zh * 4 + 2 * t, :, 128 * m : 128 * m + 128] = even[32 * zh : 32 * zh + 32]
                    c1[zh * 4 + 2 * t + 1, :, 128 * m : 128 * m + 128] = odd[32 * zh : 32 * zh + 32]
            kept = []

    def swap_x(src, dst, stage):
        return [send(src(d), dst.at[d - 1], xs.at[stage, d - 1], xr.at[stage, d - 1], at_x(d)) for d in (2, 1, 3)]

    def swap_y(src, dst, stage):
        return [send(src(d), dst.at[d - 1], ys.at[stage, d - 1], yr.at[stage, d - 1], at_y(d)) for d in (4, 3, 5, 2, 6, 1, 7)]

    def swap_z(src, dst, stage):
        return [send(src(d), dst.at[d - 1], zs.at[stage, d - 1], zr.at[stage, d - 1], at_z(d)) for d in (4, 3, 5, 2, 6, 1, 7)]

    def wait(copies):
        for copy in copies:
            copy.wait()

    def summed(own_part, parts, count):
        total = own_part.astype(F32)
        for d in range(count):
            total = total + parts[d].astype(F32)
        return total

    go_a = swap_x(lambda d: a1.at[(px + d) & 3], ra1, 0)
    go_b = swap_y(lambda d: b1.at[(py + d) & 7], rb1, 0)
    go_c = swap_z(lambda d: c1.at[(pz + d) & 7], rc1, 0)
    bias_c.wait()
    bx[0] = bc[0] + bc[1]
    go_bias = [send(bx.at[0], bx.at[d], xs.at[3, d - 1], xr.at[3, d - 1], at_x(d)) for d in (2, 1, 3)]

    eye_w = one_hot(iota((WIN, WIN), 0) == iota((WIN, WIN), 1))
    d_tok = []
    for w in range(2):
        d_qkv = nt(eye_w, dqkvt[w]).astype(BF)
        d_normed = nn(d_qkv, wt[...])
        norm = normal[WIN * w : WIN * w + WIN]
        mean_grad = jnp.mean(d_normed, axis=1, keepdims=True)
        mean_cross = jnp.mean(d_normed * norm, axis=1, keepdims=True)
        d_x = inv[WIN * w : WIN * w + WIN, 0:1] * (d_normed - mean_grad - norm * mean_cross)
        d_tok.append(d_x.astype(BF))
    for q in (3, 1, 2, 0):
        rows = slice(QROWS * q, QROWS * q + QROWS)
        give(q, nn(selt[0, rows], d_tok[0]) + nn(selt[1, rows], d_tok[1]), ot, out_tok, q + 2)

    def ordered(slots, me, n):
        total = slots[me & (n - 1)]
        for k in range(1, n):
            total = total + slots[(me - k) & (n - 1)]
        return total

    wait(go_bias)
    by[0] = ordered(bx, px, NX)
    go_bias = [send(by.at[0], by.at[d], ys.at[3, d - 1], yr.at[3, d - 1], at_y(d)) for d in (4, 3, 5, 2, 6, 1, 7)]
    wait(go_a)
    for y in range(NY):
        total = a1[px, y].astype(F32)
        for d in range(3):
            total = total + ra1[d, y].astype(F32)
        a2[y] = total.astype(BF)
    go_a = swap_y(lambda d: a2.at[(py + d) & 7], ra2, 1)
    wait(go_b)
    total = summed(b1[py], rb1, 7)
    for zh in range(2):
        for t in range(2):
            for x in range(NX):
                at = 16 * x + 8 * zh
                b2[zh * 2 + t, 8 * x : 8 * x + 8] = total[at : at + 8, 128 * t : 128 * t + 128]
    go_b = swap_z(lambda d: b2.at[((pz + d) & 7) >> 1], rb2, 1)
    wait(go_c)
    total = summed(c1[pz], rc1, 7)
    for x in range(NX):
        c2[x] = total[8 * x : 8 * x + 8]
    go_c = swap_x(lambda d: c2.at[(px + d) & 3], rc2, 1)

    wait(go_bias)
    bz[0] = ordered(by, py, NY)
    go_bias = [send(bz.at[0], bz.at[d], zs.at[3, d - 1], zr.at[3, d - 1], at_z(d)) for d in (4, 3, 5, 2, 6, 1, 7)]
    wait(go_c)
    total = summed(c2[px], rc2, 3)
    for m in range(4):
        c3[m] = total[:, 128 * m : 128 * m + 128]
    go_c = swap_y(lambda d: c3.at[((py + d) & 7) >> 1], rc3, 2)
    wait(go_b)
    total = summed(b2[pz >> 1], rb2, 7)
    for x in range(NX):
        b3[x] = total[8 * x : 8 * x + 8]
    go_b = swap_x(lambda d: b3.at[(px + d) & 3], rb3, 2)
    wait(go_a)
    total = summed(a2[py], ra2, 7)
    for zh in range(2):
        for t in range(2):
            a3[zh * 2 + t] = total[16 * zh : 16 * zh + 16, 128 * t : 128 * t + 128]
    go_a = swap_z(lambda d: a3.at[((pz + d) & 7) >> 1], ra3, 2)

    def mine(total, odd):
        return jnp.where(odd == 1, pltpu.roll(total, 64, 1), total)

    wait(go_bias)
    total = ordered(bz, pz, NZ)
    on_diagonal = iota((HEADS, 128), 0) == iota((HEADS, 128), 1)
    g_bias[...] = jnp.sum(jnp.where(on_diagonal, total, 0.0), axis=0, keepdims=True)[:, 0:HEADS]
    wait(out_sends)
    wait(go_b)
    grad_b = mine(summed(b3[px], rb3, 3), pzl & 1)
    wait(go_c)
    grad_c = mine(summed(c3[py >> 1], rc3, 7), py & 1)
    wait(go_a)
    grad_a = mine(summed(a3[pz >> 1], ra3, 7), pzl & 1)
    grads = jnp.concatenate([grad_a, grad_b, grad_c], axis=0)
    g_qkv[...] = grads[:, 0:48]
    g_out[...] = grads.T[48:64]


def place(*refs):
    count = (len(refs) - 2) // 3
    src, dst, held = refs[:count], refs[count : 2 * count], refs[2 * count : 3 * count]
    came, went = refs[-2:]
    into = [pltpu.make_async_copy(src[k], held[k], came.at[k]) for k in range(count)]
    out = [pltpu.make_async_copy(held[k], dst[k], went.at[k]) for k in range(count)]
    for copy in into:
        copy.start()
    for k in range(count):
        into[k].wait()
        out[k].start()
    for copy in out:
        copy.wait()


def cells(grid):
    return grid.transpose(1, 2, 0, 3)


def levels(grid):
    return grid.transpose(2, 0, 1, 3)


def shards(tokens, cotangent, w_qkv, w_out, land_mask, land_bias):
    vmem = pl.BlockSpec(memory_space=pltpu.VMEM)
    anywhere = pl.BlockSpec(memory_space=pl.ANY)
    V = pltpu.VMEM
    dma = pltpu.SemaphoreType.DMA
    att, tok, g_qkv, g_out, g_bias = pl.pallas_call(
        kernel,
        out_shape=[
            jax.ShapeDtypeStruct((6, 12, 4, D), BF),
            jax.ShapeDtypeStruct((6, 12, 4, D), BF),
            jax.ShapeDtypeStruct((32, 48), F32),
            jax.ShapeDtypeStruct((16, 32), F32),
            jax.ShapeDtypeStruct((1, HEADS), F32),
        ],
        in_specs=[anywhere, anywhere, anywhere, anywhere, vmem, pl.BlockSpec(memory_space=pltpu.SMEM)],
        out_specs=[vmem] * 5,
        scratch_shapes=[
            V((6, 12, 4, D), BF), V((6, 12, 4, D), BF), V((4, 18, 8, D), F32),
            V((3, 3, 6, 4, D), BF), V((3, 3, 6, 4, D), BF),
            V((2, HEADS, WIN, WIN), F32), V((2, HEADS, WIN, WIN), BF),
            V((2, HEADS, WIN, WIN), BF), V((2, HEADS, WIN, WIN), BF),
            V((2, HEADS, HD + 16, WIN), BF), V((2, HEADS, HD + 16, WIN), BF),
            V((D, 3 * D), BF), V((D, D), BF), V((3 * D, D), BF),
            V((D, D), BF), V((2 * WIN, 4 * QROWS), BF), V((2, 4 * QROWS, WIN), BF),
            V((2 * WIN, D), F32), V((2 * WIN, 128), F32),
            V((2 * WIN, D), BF), V((2 * WIN, D), BF),
            V((2, D, WIN), BF), V((2, D, WIN), BF), V((2, D, WIN), BF),
            V((2, D, WIN), BF), V((2, D, WIN), BF), V((2, 3 * D, WIN), BF),
            V((2, 4 * D, WIN), BF), V((2, 4 * D, WIN), BF),
            V((3, 3, 6, 4, D), BF), V((3, 3, 6, 4, D), BF),
            V((NY, 256, 256), BF), V((NY, 256, 256), BF),
            V((NX, NY, 32, 256), BF), V((3, NY, 32, 256), BF),
            V((NY, 32, 256), BF), V((7, 32, 256), BF),
            V((4, 16, 128), F32), V((7, 16, 128), F32),
            V((NY, 64, 256), BF), V((7, 64, 256), BF),
            V((4, 32, 128), F32), V((7, 32, 128), F32),
            V((NX, 8, 128), F32), V((3, 8, 128), F32),
            V((NZ, 32, 512), BF), V((7, 32, 512), BF),
            V((NX, 8, 512), F32), V((3, 8, 512), F32),
            V((4, 8, 128), F32), V((7, 8, 128), F32),
            V((2, HEADS, WIN), F32), V((2, HEADS, 128), F32),
            V((NX, HEADS, 128), F32), V((NY, HEADS, 128), F32), V((NZ, HEADS, 128), F32),
            dma((4,)), dma((6,)), dma((6,)), dma((6,)), dma((6,)),
            dma((5,)), dma((5,)),
            dma((4, 3)), dma((4, 3)), dma((4, 7)), dma((4, 7)), dma((4, 7)), dma((4, 7)),
        ],
        compiler_params=pltpu.CompilerParams(
            collective_id=0, has_side_effects=True, vmem_limit_bytes=60 << 20
        ),
        name="swin_block",
    )(cells(tokens), cells(cotangent), w_qkv, w_out, land_mask, land_bias)
    results = (att, tok, g_qkv, g_out, g_bias)
    att, tok, g_qkv, g_out, g_bias = pl.pallas_call(
        place,
        out_shape=[jax.ShapeDtypeStruct(x.shape, x.dtype) for x in results],
        in_specs=[anywhere] * 5,
        out_specs=[anywhere] * 5,
        scratch_shapes=[V(x.shape, x.dtype) for x in results] + [dma((5,)), dma((5,))],
        compiler_params=pltpu.CompilerParams(vmem_limit_bytes=60 << 20),
        name="place",
    )(*results)
    return levels(att), levels(tok), g_qkv, g_out.T, g_bias.reshape(HEADS)


def solution(mesh):
    in_specs = (P(None, "lat", "lon", None), P(None, "lat", "lon", None), P(), P(), P(), P())
    out_specs = (
        P(None, "lat", "lon", None),
        P(None, "lat", "lon", None),
        P("lat", "lon"),
        P("lat", "lon"),
        P(),
    )
    return jax.shard_map(shards, mesh=mesh, in_specs=in_specs, out_specs=out_specs, check_vma=False)
```

```python
import jax
import jax.numpy as jnp
from jax import lax
from jax.experimental import pallas as pl
from jax.experimental.pallas import tpu as pltpu
from jax.sharding import PartitionSpec as P

MESH = pl.DeviceIdType.MESH
BF = jnp.bfloat16
F32 = jnp.float32
D = 512
HEADS = 8
HD = 64
WIN = 144
QROWS = 18 * 8
NX, NY, NZ = 4, 8, 8


def nn(a, b):
    return lax.dot_general(a, b, (((1,), (0,)), ((), ())), preferred_element_type=F32)


def nt(a, b):
    return lax.dot_general(a, b, (((1,), (1,)), ((), ())), preferred_element_type=F32)


def tn(a, b):
    return lax.dot_general(a, b, (((0,), (0,)), ((), ())), preferred_element_type=F32)


def iota(shape, axis):
    return lax.broadcasted_iota(jnp.int32, shape, axis)


def one_hot(cond):
    return jnp.where(cond, 1.0, 0.0).astype(BF)


def token_place(t):
    quad = (t >= 36).astype(jnp.int32) + (t >= 72).astype(jnp.int32) + (t >= 108).astype(jnp.int32)
    rem = t - 36 * quad
    lev = (rem >= 18).astype(jnp.int32)
    pos = rem - 18 * lev
    row = (pos >= 6).astype(jnp.int32) + (pos >= 12).astype(jnp.int32)
    return quad, lev, row, pos - 6 * row


def quad_row(s):
    w = (s >= WIN).astype(jnp.int32)
    quad, lev, row, col = token_place(s - WIN * w)
    return quad * QROWS + (row * 6 + col) * 8 + ((2 * w + lev + 1) & 3)


def kernel(
    tok_h, cot_h, wqkv_h, wout_h, land, bias,
    out_att, out_tok, g_qkv, g_out, g_bias,
    tok_v, cot_v, padded, hx, hc, probs, prob_b, d_prob, d_score, ka, qa,
    wqkv, wout, wt, perm, sel, selt, normal, inv,
    normw, cotw, nmt, vt, dmt, mixt, mixp, dqkvt, r_q, r_o,
    oa, ot, core_s, core_r, own,
    a1, ra1, a2, ra2, a3, ra3, b1, rb1, b2, rb2, b3, rb3, c1, rc1, c2, rc2, c3, rc3,
    dbias, bc, bx, by, bz,
    lsem, hs, hr, os, orr, cs, cr, xs, xr, ys, yr, zs, zr,
):
    lat = lax.axis_index("lat")
    lon = lax.axis_index("lon")
    core = lat & 1
    px = (lat >> 1) & 3
    pzh = lat >> 3
    py = lon >> 2
    pzl = lon & 3
    pz = pzh * 4 + pzl

    def dev(x, y, z, c):
        return ((z >> 2) * 8 + x * 2 + c, y * 4 + (z & 3))

    def at_core():
        return dev(px, py, pz, 1 - core)

    def at_x(d):
        return dev((px + d) & 3, py, pz, core)

    def at_y(d):
        return dev(px, (py + d) & 7, pz, core)

    def at_z(d):
        return dev(px, py, (pz + d) & 7, core)

    back = [None, ((lat + 15) & 15, lon), (lat, (lon + 31) & 31), ((lat + 15) & 15, (lon + 31) & 31)]
    ahead = [None, ((lat + 1) & 15, lon), (lat, (lon + 1) & 31), ((lat + 1) & 15, (lon + 1) & 31)]

    barrier = pltpu.get_barrier_semaphore()
    partners = back[1:] + ahead[1:] + [at_core()]
    partners += [at_x(d) for d in range(1, NX)]
    partners += [at_y(d) for d in range(1, NY)] + [at_z(d) for d in range(1, NZ)]
    for where in partners:
        pl.semaphore_signal(barrier, inc=1, device_id=where, device_id_type=MESH)

    t_copy = pltpu.make_async_copy(tok_h, tok_v, lsem.at[2])
    t_copy.start()
    c_copy = pltpu.make_async_copy(cot_h, cot_v, lsem.at[3])
    c_copy.start()
    w_copy = pltpu.make_async_copy(wqkv_h, wqkv, lsem.at[0])
    w_copy.start()
    o_copy = pltpu.make_async_copy(wout_h, wout, lsem.at[1])
    o_copy.start()
    t_copy.wait()
    c_copy.wait()
    pl.semaphore_wait(barrier, len(partners))

    def send(src, dst, ssem, rsem, where):
        copy = pltpu.make_async_remote_copy(
            src_ref=src, dst_ref=dst, send_sem=ssem, recv_sem=rsem,
            device_id=where, device_id_type=MESH,
        )
        copy.start()
        return copy

    places = [(slice(3 - 3 * (q & 1), 6 - 3 * (q & 1)), slice(6 - 6 * (q >> 1), 12 - 6 * (q >> 1))) for q in range(4)]

    def halo(held, far, first):
        return [
            send(held.at[places[q]], far.at[q - 1], hs.at[first + q - 1], hr.at[first + q - 1], back[q])
            for q in (3, 1, 2)
        ]

    halo_x = halo(tok_v, hx, 0)
    halo_c = halo(cot_v, hc, 3)

    padded[...] = jnp.zeros_like(padded)
    s_col = iota((2 * WIN, 1), 0)
    sel[...] = one_hot(iota((2 * WIN, 4 * QROWS), 1) == quad_row(s_col))
    for w in range(2):
        s_row = iota((1, WIN), 1) + w * WIN
        selt[w] = one_hot(iota((4 * QROWS, WIN), 0) == quad_row(s_row))
    r = iota((D, 1), 0)
    half = r >> 8
    a = r & 255
    is_a = a < 128
    is_b = a < 192
    b = a & 63
    f_x = jnp.where(is_a, a >> 5, jnp.where(is_b, b >> 4, (b >> 3) & 3))
    f_zh = jnp.where(is_a, (a >> 4) & 1, jnp.where(is_b, (b >> 3) & 1, b >> 5))
    f_i = jnp.where(is_a, a & 15, jnp.where(is_b, 16 + (b & 7), 24 + (b & 7)))
    f_c = jnp.where(half == 0, 1 - core, core)
    perm[...] = one_hot(iota((D, D), 1) == f_zh * 256 + f_x * 64 + f_c * 32 + f_i)

    r_q[...] = jnp.zeros_like(r_q)
    r_o[...] = jnp.zeros_like(r_o)

    quad, _, row, col = token_place(iota((1, WIN), 1))
    l_row = lat * 6 + 3 + (quad & 1) * 3 + row
    l_row = jnp.where(l_row >= 96, l_row - 96, l_row)
    l_col = lon * 12 + 6 + (quad >> 1) * 6 + col
    l_col = jnp.where(l_col >= 384, l_col - 384, l_col)
    picked = nn(land[...].astype(F32).astype(BF), one_hot(iota((384, WIN), 0) == l_col))
    land_key = jnp.sum(jnp.where(iota((96, WIN), 0) == l_row, picked, 0.0), axis=0, keepdims=True)

    extra = iota((16, WIN), 0)
    is_land = (extra >= 4) & (extra < 7)
    for w in range(2):
        quad, lev, _, _ = token_place(iota((16, WIN), 1))
        region = jnp.where(lat == 15, 2, 0) * (quad & 1) + (lev if w == 1 else 0)
        here = extra == region
        under_keys = jnp.where(here, 1.0, jnp.where(is_land, land_key, 0.0)).astype(BF)
        barred = jnp.where(here | (extra >= 4), 0.0, -1e30)
        for h in range(HEADS):
            full = jnp.zeros((16, WIN), F32) + bias[h]
            first = full.astype(BF).astype(F32)
            second = (full - first).astype(BF).astype(F32)
            third = full - first - second
            pieces = jnp.where(extra == 4, first, jnp.where(extra == 5, second, third))
            ka[w, h, HD : HD + 16] = under_keys
            qa[w, h, HD : HD + 16] = jnp.where(is_land, pieces, barred).astype(BF)

    w_copy.wait()
    o_copy.wait()
    eye = one_hot(iota((256, 256), 0) == iota((256, 256), 1))
    for k in range(6):
        wt[256 * k : 256 * k + 256] = nt(eye, wqkv[:, 256 * k : 256 * k + 256]).astype(BF)

    def gather(own, far, copies):
        padded[0, :, 0:4] = own[places[0]].reshape(18, 4, D).astype(F32)
        for copy, q in zip(copies, (3, 1, 2)):
            copy.wait()
            padded[q, :, 0:4] = far[q - 1].reshape(18, 4, D).astype(F32)
        return nn(sel[...], padded[...].reshape(4 * QROWS, D).astype(BF))

    x = gather(tok_v, hx, halo_x)
    centred = x - jnp.mean(x, axis=1, keepdims=True)
    scale = lax.rsqrt(jnp.mean(centred * centred, axis=1, keepdims=True) + 1e-05)
    normal[...] = centred * scale
    inv[...] = jnp.broadcast_to(scale, (2 * WIN, 128))
    normw[...] = normal[...].astype(BF)
    for w in range(2):
        nw = normw[WIN * w : WIN * w + WIN]
        qkv = nt(wt[...], nw).astype(BF)
        for h in range(HEADS):
            qa[w, h, 0:HD] = qkv[h * HD : h * HD + HD] * (HD ** -0.5)
            ka[w, h, 0:HD] = qkv[D + h * HD : D + h * HD + HD]
        vt[w] = qkv[2 * D :]
        nmt[w] = nt(perm[...], nw).astype(BF)
    pairs = [(w, h) for h in range(HEADS) for w in range(2)]

    def head(h):
        return slice(h * HD, h * HD + HD)

    for w, h in pairs:
        probs[w, h] = tn(ka[w, h], qa[w, h])
    for w, h in pairs:
        score = probs[w, h]
        expo = jnp.exp(score - jnp.max(score, axis=0, keepdims=True))
        prob = expo * (1.0 / jnp.sum(expo, axis=0, keepdims=True))
        probs[w, h] = prob
        prob_b[w, h] = prob.astype(BF)
    for w, h in pairs:
        mixt[w, head(h)] = nn(vt[w, head(h)], prob_b[w, h]).astype(BF)

    out_sends = []

    def give(q, value, away, far, k):
        value = value.reshape(18, 8, D)[:, 0:4].reshape(3, 6, 4, D).astype(BF)
        if q == 0:
            far[places[0]] = value
        else:
            away[q - 1] = value
            out_sends.append(send(away.at[q - 1], far.at[places[q]], os.at[k], orr.at[k], ahead[q]))

    for q in (3, 1, 2, 0):
        rows = slice(QROWS * q, QROWS * q + QROWS)
        mixed = (nt(selt[0, rows], mixt[0]) + nt(selt[1, rows], mixt[1])).astype(BF)
        give(q, nn(mixed, wout[...]), oa, out_att, q - 1)

    cotw[...] = gather(cot_v, hc, halo_c).astype(BF)
    for w in range(2):
        cw = cotw[WIN * w : WIN * w + WIN]
        dmt[w] = nt(wout[...], cw).astype(BF)
        for k in range(2):
            ct = nt(eye, cw[:, 256 * k : 256 * k + 256]).astype(BF)
            for g in range(16):
                at = 64 * (16 * k + g) + 48
                r_o[w, at : at + 16] = ct[16 * g : 16 * g + 16]

    for w, h in pairs:
        d_prob[w, h] = tn(vt[w, head(h)], dmt[w, head(h)]).astype(BF)

    def keep(w, h, k, grad):
        dqkvt[w, k * D + h * HD : k * D + h * HD + HD] = grad
        for g in range(4):
            piece = h * 4 + k * 32 + g
            at = (piece // 3) * 64 + (piece % 3) * 16
            r_q[w, at : at + 16] = grad[16 * g : 16 * g + 16]

    for w, h in pairs:
        keep(w, h, 2, nt(dmt[w, head(h)], prob_b[w, h]).astype(BF))
    for w, h in pairs:
        prob = probs[w, h]
        dp = d_prob[w, h].astype(F32)
        d_score[w, h] = (prob * (dp - jnp.sum(prob * dp, axis=0, keepdims=True))).astype(BF)
    for w, h in pairs:
        under = nn(ka[w, h], d_score[w, h])
        keep(w, h, 0, (under[0:HD] * (HD ** -0.5)).astype(BF))
        dbias[w, h : h + 1] = under[HD + 4 : HD + 5]
        keep(w, h, 1, nt(qa[w, h, 0:HD], d_score[w, h]).astype(BF))

    bc[0] = jnp.broadcast_to(jnp.sum(dbias[0] + dbias[1], axis=1, keepdims=True), (HEADS, 128))
    bias_c = send(bc.at[0], bc.at[1], cs.at[0], cr.at[0], at_core())

    for w in range(2):
        mixp[w] = nn(perm[...], mixt[w]).astype(BF)

    def grad_block(first, y):
        cols = slice(y * 256, y * 256 + 256)
        total = None
        for w in range(2):
            for left, right in ((nmt, r_q), (mixp, r_o)):
                term = nt(left[w, first : first + 256], right[w, cols])
                total = term if total is None else total + term
        return total

    core_copies = []
    for y in range(NY):
        core_s[y] = grad_block(0, y).astype(BF)
        if y % 4 == 3:
            group, k = slice(y - 3, y + 1), 1 + y // 4
            core_copies.append(send(core_s.at[group], core_r.at[group], cs.at[k], cr.at[k], at_core()))

    for y in range(NY):
        own[y] = grad_block(256, y)
    lane_low = iota((64, 128), 1) < 64
    kept = []
    for y in range(NY):
        if y % 4 == 0:
            core_copies[y // 4].wait()
        total = own[y] + core_r[y].astype(F32)
        for x in range(NX):
            a1[x, y] = total[32 * x : 32 * x + 32].astype(BF)
        b1[y] = total[128:192].astype(BF)
        kept.append(total[192:256])
        if y % 2 == 1:
            m = y // 2
            for t in range(2):
                lo = kept[0][:, 128 * t : 128 * t + 128]
                hi = kept[1][:, 128 * t : 128 * t + 128]
                even = jnp.where(lane_low, lo, pltpu.roll(hi, 64, 1)).astype(BF)
                odd = jnp.where(lane_low, pltpu.roll(lo, 64, 1), hi).astype(BF)
                for zh in range(2):
                    c1[zh * 4 + 2 * t, :, 128 * m : 128 * m + 128] = even[32 * zh : 32 * zh + 32]
                    c1[zh * 4 + 2 * t + 1, :, 128 * m : 128 * m + 128] = odd[32 * zh : 32 * zh + 32]
            kept = []

    def swap_x(src, dst, stage):
        return [send(src(d), dst.at[d - 1], xs.at[stage, d - 1], xr.at[stage, d - 1], at_x(d)) for d in (2, 1, 3)]

    def swap_y(src, dst, stage):
        return [send(src(d), dst.at[d - 1], ys.at[stage, d - 1], yr.at[stage, d - 1], at_y(d)) for d in (4, 3, 5, 2, 6, 1, 7)]

    def swap_z(src, dst, stage):
        return [send(src(d), dst.at[d - 1], zs.at[stage, d - 1], zr.at[stage, d - 1], at_z(d)) for d in (4, 3, 5, 2, 6, 1, 7)]

    def wait(copies):
        for copy in copies:
            copy.wait()

    def summed(own_part, parts, count):
        total = own_part.astype(F32)
        for d in range(count):
            total = total + parts[d].astype(F32)
        return total

    go_a = swap_x(lambda d: a1.at[(px + d) & 3], ra1, 0)
    go_b = swap_y(lambda d: b1.at[(py + d) & 7], rb1, 0)
    go_c = swap_z(lambda d: c1.at[(pz + d) & 7], rc1, 0)
    bias_c.wait()
    bx[0] = bc[0] + bc[1]
    go_bias = [send(bx.at[0], bx.at[d], xs.at[3, d - 1], xr.at[3, d - 1], at_x(d)) for d in (2, 1, 3)]

    eye_w = one_hot(iota((WIN, WIN), 0) == iota((WIN, WIN), 1))
    d_tok = []
    for w in range(2):
        d_qkv = nt(eye_w, dqkvt[w]).astype(BF)
        d_normed = nn(d_qkv, wt[...])
        norm = normal[WIN * w : WIN * w + WIN]
        mean_grad = jnp.mean(d_normed, axis=1, keepdims=True)
        mean_cross = jnp.mean(d_normed * norm, axis=1, keepdims=True)
        d_x = inv[WIN * w : WIN * w + WIN, 0:1] * (d_normed - mean_grad - norm * mean_cross)
        d_tok.append(d_x.astype(BF))
    for q in (3, 1, 2, 0):
        rows = slice(QROWS * q, QROWS * q + QROWS)
        give(q, nn(selt[0, rows], d_tok[0]) + nn(selt[1, rows], d_tok[1]), ot, out_tok, q + 2)

    def ordered(slots, me, n):
        total = slots[me & (n - 1)]
        for k in range(1, n):
            total = total + slots[(me - k) & (n - 1)]
        return total

    wait(go_bias)
    by[0] = ordered(bx, px, NX)
    go_bias = [send(by.at[0], by.at[d], ys.at[3, d - 1], yr.at[3, d - 1], at_y(d)) for d in (4, 3, 5, 2, 6, 1, 7)]
    wait(go_a)
    for y in range(NY):
        total = a1[px, y].astype(F32)
        for d in range(3):
            total = total + ra1[d, y].astype(F32)
        a2[y] = total.astype(BF)
    go_a = swap_y(lambda d: a2.at[(py + d) & 7], ra2, 1)
    wait(go_b)
    total = summed(b1[py], rb1, 7)
    for zh in range(2):
        for t in range(2):
            for x in range(NX):
                at = 16 * x + 8 * zh
                b2[zh * 2 + t, 8 * x : 8 * x + 8] = total[at : at + 8, 128 * t : 128 * t + 128]
    go_b = swap_z(lambda d: b2.at[((pz + d) & 7) >> 1], rb2, 1)
    wait(go_c)
    total = summed(c1[pz], rc1, 7)
    for x in range(NX):
        c2[x] = total[8 * x : 8 * x + 8]
    go_c = swap_x(lambda d: c2.at[(px + d) & 3], rc2, 1)

    wait(go_bias)
    bz[0] = ordered(by, py, NY)
    go_bias = [send(bz.at[0], bz.at[d], zs.at[3, d - 1], zr.at[3, d - 1], at_z(d)) for d in (4, 3, 5, 2, 6, 1, 7)]
    wait(go_c)
    total = summed(c2[px], rc2, 3)
    for m in range(4):
        c3[m] = total[:, 128 * m : 128 * m + 128]
    go_c = swap_y(lambda d: c3.at[((py + d) & 7) >> 1], rc3, 2)
    wait(go_b)
    total = summed(b2[pz >> 1], rb2, 7)
    for x in range(NX):
        b3[x] = total[8 * x : 8 * x + 8]
    go_b = swap_x(lambda d: b3.at[(px + d) & 3], rb3, 2)
    wait(go_a)
    total = summed(a2[py], ra2, 7)
    for zh in range(2):
        for t in range(2):
            a3[zh * 2 + t] = total[16 * zh : 16 * zh + 16, 128 * t : 128 * t + 128]
    go_a = swap_z(lambda d: a3.at[((pz + d) & 7) >> 1], ra3, 2)

    def mine(total, odd):
        return jnp.where(odd == 1, pltpu.roll(total, 64, 1), total)

    wait(go_bias)
    total = ordered(bz, pz, NZ)
    on_diagonal = iota((HEADS, 128), 0) == iota((HEADS, 128), 1)
    g_bias[...] = jnp.sum(jnp.where(on_diagonal, total, 0.0), axis=0, keepdims=True)[:, 0:HEADS]
    wait(out_sends)
    wait(go_b)
    grad_b = mine(summed(b3[px], rb3, 3), pzl & 1)
    wait(go_c)
    grad_c = mine(summed(c3[py >> 1], rc3, 7), py & 1)
    wait(go_a)
    grad_a = mine(summed(a3[pz >> 1], ra3, 7), pzl & 1)
    grads = jnp.concatenate([grad_a, grad_b, grad_c], axis=0)
    g_qkv[...] = grads[:, 0:48]
    g_out[...] = grads.T[48:64]


def place(*refs):
    count = (len(refs) - 2) // 3
    src, dst, held = refs[:count], refs[count : 2 * count], refs[2 * count : 3 * count]
    came, went = refs[-2:]
    into = [pltpu.make_async_copy(src[k], held[k], came.at[k]) for k in range(count)]
    out = [pltpu.make_async_copy(held[k], dst[k], went.at[k]) for k in range(count)]
    for copy in into:
        copy.start()
    for k in range(count):
        into[k].wait()
        out[k].start()
    for copy in out:
        copy.wait()


def cells(grid):
    return grid.transpose(1, 2, 0, 3)


def levels(grid):
    return grid.transpose(2, 0, 1, 3)


def shards(tokens, cotangent, w_qkv, w_out, land_mask, land_bias):
    vmem = pl.BlockSpec(memory_space=pltpu.VMEM)
    anywhere = pl.BlockSpec(memory_space=pl.ANY)
    V = pltpu.VMEM
    dma = pltpu.SemaphoreType.DMA
    att, tok, g_qkv, g_out, g_bias = pl.pallas_call(
        kernel,
        out_shape=[
            jax.ShapeDtypeStruct((6, 12, 4, D), BF),
            jax.ShapeDtypeStruct((6, 12, 4, D), BF),
            jax.ShapeDtypeStruct((32, 48), F32),
            jax.ShapeDtypeStruct((16, 32), F32),
            jax.ShapeDtypeStruct((1, HEADS), F32),
        ],
        in_specs=[anywhere, anywhere, anywhere, anywhere, vmem, pl.BlockSpec(memory_space=pltpu.SMEM)],
        out_specs=[vmem] * 5,
        scratch_shapes=[
            V((6, 12, 4, D), BF), V((6, 12, 4, D), BF), V((4, 18, 8, D), F32),
            V((3, 3, 6, 4, D), BF), V((3, 3, 6, 4, D), BF),
            V((2, HEADS, WIN, WIN), F32), V((2, HEADS, WIN, WIN), BF),
            V((2, HEADS, WIN, WIN), BF), V((2, HEADS, WIN, WIN), BF),
            V((2, HEADS, HD + 16, WIN), BF), V((2, HEADS, HD + 16, WIN), BF),
            V((D, 3 * D), BF), V((D, D), BF), V((3 * D, D), BF),
            V((D, D), BF), V((2 * WIN, 4 * QROWS), BF), V((2, 4 * QROWS, WIN), BF),
            V((2 * WIN, D), F32), V((2 * WIN, 128), F32),
            V((2 * WIN, D), BF), V((2 * WIN, D), BF),
            V((2, D, WIN), BF), V((2, D, WIN), BF), V((2, D, WIN), BF),
            V((2, D, WIN), BF), V((2, D, WIN), BF), V((2, 3 * D, WIN), BF),
            V((2, 4 * D, WIN), BF), V((2, 4 * D, WIN), BF),
            V((3, 3, 6, 4, D), BF), V((3, 3, 6, 4, D), BF),
            V((NY, 256, 256), BF), V((NY, 256, 256), BF), V((NY, 256, 256), F32),
            V((NX, NY, 32, 256), BF), V((3, NY, 32, 256), BF),
            V((NY, 32, 256), BF), V((7, 32, 256), BF),
            V((4, 16, 128), F32), V((7, 16, 128), F32),
            V((NY, 64, 256), BF), V((7, 64, 256), BF),
            V((4, 32, 128), F32), V((7, 32, 128), F32),
            V((NX, 8, 128), F32), V((3, 8, 128), F32),
            V((NZ, 32, 512), BF), V((7, 32, 512), BF),
            V((NX, 8, 512), F32), V((3, 8, 512), F32),
            V((4, 8, 128), F32), V((7, 8, 128), F32),
            V((2, HEADS, WIN), F32), V((2, HEADS, 128), F32),
            V((NX, HEADS, 128), F32), V((NY, HEADS, 128), F32), V((NZ, HEADS, 128), F32),
            dma((4,)), dma((6,)), dma((6,)), dma((6,)), dma((6,)),
            dma((5,)), dma((5,)),
            dma((4, 3)), dma((4, 3)), dma((4, 7)), dma((4, 7)), dma((4, 7)), dma((4, 7)),
        ],
        compiler_params=pltpu.CompilerParams(
            collective_id=0, has_side_effects=True, vmem_limit_bytes=60 << 20
        ),
        name="swin_block",
    )(cells(tokens), cells(cotangent), w_qkv, w_out, land_mask, land_bias)
    results = (att, tok, g_qkv, g_out, g_bias)
    att, tok, g_qkv, g_out, g_bias = pl.pallas_call(
        place,
        out_shape=[jax.ShapeDtypeStruct(x.shape, x.dtype) for x in results],
        in_specs=[anywhere] * 5,
        out_specs=[anywhere] * 5,
        scratch_shapes=[V(x.shape, x.dtype) for x in results] + [dma((5,)), dma((5,))],
        compiler_params=pltpu.CompilerParams(vmem_limit_bytes=60 << 20),
        name="place",
    )(*results)
    return levels(att), levels(tok), g_qkv, g_out.T, g_bias.reshape(HEADS)


def solution(mesh):
    in_specs = (P(None, "lat", "lon", None), P(None, "lat", "lon", None), P(), P(), P(), P())
    out_specs = (
        P(None, "lat", "lon", None),
        P(None, "lat", "lon", None),
        P("lat", "lon"),
        P("lat", "lon"),
        P(),
    )
    return jax.shard_map(shards, mesh=mesh, in_specs=in_specs, out_specs=out_specs, check_vma=False)
```
